32 devices in a mesh: row: 4 (over y, x), col: 8 (over z, core).
Axes of the slice: x: 2, y: 2, z: 4, core: 2. Of those that a mesh axis runs over, the one named last changes fastest.
Arguments:
- start_block: float32 [96, 256, 1024], P(None, 'row', 'col'), may hold values from -6 to 6
- stiffness: float32 [256, 1024], P('row', 'col'), may hold values from 0.5 to 2
Outputs:
- basis: float32 [96, 256, 1024], P(None, 'row', 'col')
- projected: float32 [96, 96], replicated
The draws below stay inside these ranges and needn't reach their ends.
All inputs are finite; a program needn't handle non-finite values.
Results may differ from the reference program's by a relative error of at most 0.000086.
Values sent between devices are 32-bit elements; how exact they have to be, the bound alone decides.
No kernel may reach another device: no remote copies, remote signals or barrier semaphores. Data moves between devices by JAX's collectives and lax.ppermute only.
A program may use at most 64 MiB of HBM per device.

```python
import math
import jax
import jax.numpy as jnp
from jax import lax

K = 96
DEGREE = 4
NX = 256
NY = 1024


def level_of(rng, shape, split, least, top_value):
    def one(axis_at, shards_of):
        draws = jax.random.uniform(jax.random.fold_in(jax.random.fold_in(rng, 6), axis_at), (shards_of,), jnp.float32, least / len(split), top_value / len(split))
        return jnp.repeat(jnp.exp(draws), shape[axis_at] // shards_of).reshape((-1,) + (1,) * (len(shape) - axis_at - 1))

    loudness = one(*split[0])
    for cut in split[1:]:
        loudness = loudness * one(*cut)
    return loudness


def bell_draw(key, extent, spread, limit, pieces=(), kind=jnp.bfloat16):
    loudness = level_of(key, extent, pieces, -0.22, 0.18) if pieces else 1.0
    array = jax.random.normal(key, extent, jnp.float32) * spread * loudness
    return jnp.minimum(jnp.maximum(array, -limit), limit).astype(kind)


def setup_inputs(seed: int = 0) -> dict:
    keys = jax.random.split(jax.random.key(seed), 3)
    start_block = bell_draw(keys[0], (K, NX, NY), 1.0, 6.0, ((1, 4), (2, 8)), jnp.float32)
    stiffness = jnp.clip(jnp.exp(math.log(2.0) - 1.3862944 * jax.random.uniform(keys[1], (NX, NY), jnp.float32) ** level_of(keys[1], (NX, NY), ((0, 4), (1, 8)), -0.2, 0.2)), 0.5, 2.0)
    return dict(start_block=start_block, stiffness=stiffness)


TOP = 129.0
CUT = 16.0
SHIFT = 1.0

def stencil(padded):
    return 4.0 * padded[:, 1:-1, 1:-1] - (padded[:, 2:, 1:-1] + padded[:, :-2, 1:-1] + padded[:, 1:-1, 2:] + padded[:, 1:-1, :-2])

def pad_one(field):
    return jnp.pad(field, ((0, 0), (1, 1), (1, 1)))

def operate(field, stiffness):
    return stencil(pad_one(stiffness * stencil(pad_one(field)))) + SHIFT * field

def chebyshev(block, stiffness):
    center = (TOP + CUT) / 2.0
    half = (TOP - CUT) / 2.0
    previous = block
    current = (center * block - operate(block, stiffness)) / half
    for step in range(DEGREE - 1):
        nxt = 2.0 * (center * current - operate(current, stiffness)) / half - previous
        previous, current = (current, nxt)
    return current

def reference(start_block, stiffness):
    groups = start_block.reshape(K // 8, 8, NX, NY)
    filtered_groups = lax.map(lambda part: chebyshev(part, stiffness), groups)
    flat = filtered_groups.reshape(K, NX * NY)
    gram = jnp.dot(flat.astype(jnp.float32), flat.T.astype(jnp.float32), preferred_element_type=jnp.float32, precision=lax.Precision.HIGHEST)

    def image_rows(part):
        image = operate(part, stiffness).reshape(8, NX * NY)
        return jnp.dot(image.astype(jnp.float32), flat.T.astype(jnp.float32), preferred_element_type=jnp.float32, precision=lax.Precision.HIGHEST)
    image_gram = lax.map(image_rows, filtered_groups).reshape(K, K)
    factor = jnp.linalg.cholesky(gram)
    ortho = lax.linalg.triangular_solve(factor, flat, left_side=True, lower=True)
    basis = (jnp.sqrt(jnp.float32(NX * NY)) * ortho).reshape(K, NX, NY)
    middle = lax.linalg.triangular_solve(factor, image_gram, left_side=True, lower=True)
    projected = lax.linalg.triangular_solve(factor, middle.T, left_side=True, lower=True).T
    return (basis, projected / TOP)
```

```python
import functools
import jax
import jax.numpy as jnp
from jax import lax
from jax.experimental import pallas as pl
from jax.experimental.pallas import tpu as pltpu
from jax.sharding import PartitionSpec as P

DEGREE = 4
TOP = 129.0
CUT = 16.0
SHIFT = 1.0
CENTER = (TOP + CUT) / 2.0
HALF = (TOP - CUT) / 2.0
HALO = 2 * DEGREE + 1
LANES = 128
PAD = 16
F32 = jnp.float32
BF16 = jnp.bfloat16
MIB = 2**20


def split(values):
    high = values.astype(BF16)
    low = (values - high.astype(F32)).astype(BF16)
    return high, low


def even(index):
    return lax.rem(index, 2) == 0


def turn_kernel(block_ref, stiff_ref, cells_ref, near_ref, far_ref):
    vectors, rows, cols = block_ref.shape
    first = even(lax.axis_index("col"))
    fill = jnp.zeros((LANES - vectors - 8, cols), F32)
    for x in range(rows):
        stiff = jnp.broadcast_to(stiff_ref[x : x + 1, :], (8, cols))
        turned = jnp.concatenate([block_ref[:, x, :], stiff, fill], axis=0).T
        cells_ref[x] = turned
        head, tail = turned[:HALO], turned[cols - HALO :]
        near_ref[x * HALO : (x + 1) * HALO, :] = jnp.where(first, tail, head)
        far_ref[x * HALO : (x + 1) * HALO, :] = jnp.where(first, head, tail)


def turn(block, stiffness):
    vectors, rows, cols = block.shape
    step = 8
    slab = jax.ShapeDtypeStruct((rows * HALO, LANES), F32)
    slab_spec = pl.BlockSpec((step * HALO, LANES), lambda i: (i, 0))
    return pl.pallas_call(
        turn_kernel,
        grid=(rows // step,),
        in_specs=[
            pl.BlockSpec((vectors, step, cols), lambda i: (0, i, 0)),
            pl.BlockSpec((step, cols), lambda i: (i, 0)),
        ],
        out_specs=[pl.BlockSpec((step, cols, LANES), lambda i: (i, 0, 0)), slab_spec, slab_spec],
        out_shape=[jax.ShapeDtypeStruct((rows, cols, LANES), F32), slab, slab],
        compiler_params=pltpu.CompilerParams(vmem_limit_bytes=32 * MIB),
    )(block, stiffness)


def edge_kernel(cells_ref, near_ref, far_ref, one_ref, two_ref, sem):
    rows, cols, _ = cells_ref.shape
    margin = HALO - 1
    col_first = even(lax.axis_index("col"))
    row_first = even(lax.axis_index("row"))

    def fill(out_ref, start):
        copy = pltpu.make_async_copy(
            cells_ref.at[pl.ds(start, HALO)], out_ref.at[:, pl.ds(margin, cols), :], sem
        )
        copy.start()
        for x in range(HALO):
            base = (start + x) * HALO
            near = near_ref[pl.ds(base, HALO), :]
            far = far_ref[pl.ds(base, HALO), :]
            left = jnp.where(col_first, far, near)
            right = jnp.where(col_first, near, far)
            out_ref[x, :margin, :] = left[HALO - margin :]
            out_ref[x, margin + cols :, :] = right[:margin]
        copy.wait()

    fill(one_ref, jnp.where(row_first, rows - HALO, 0))
    fill(two_ref, jnp.where(row_first, 0, rows - HALO))


def edges(cells, near, far):
    rows, cols, _ = cells.shape
    vmem = pl.BlockSpec(memory_space=pltpu.VMEM)
    slab = jax.ShapeDtypeStruct((HALO, cols + 2 * HALO - 2, LANES), F32)
    return pl.pallas_call(
        edge_kernel,
        in_specs=[pl.BlockSpec(memory_space=pl.ANY), vmem, vmem],
        out_specs=[vmem, vmem],
        out_shape=[slab, slab],
        scratch_shapes=[pltpu.SemaphoreType.DMA],
        compiler_params=pltpu.CompilerParams(vmem_limit_bytes=32 * MIB),
    )(cells, near, far)


def filter_kernel(vectors, cells_ref, near_ref, far_ref, one_ref, two_ref, turned_ref, sums_ref,
                  even_field, odd_field, inner, stiff, turned, sums, in_sems, out_sem):
    rows, cols, _ = cells_ref.shape
    margin = HALO - 1
    row, row_count = lax.axis_index("row"), lax.axis_size("row")
    col, col_count = lax.axis_index("col"), lax.axis_size("col")
    col_first, row_first = even(col), even(row)
    wide = pl.ds(PAD - margin, cols + 2 * margin)
    tiles = range(PAD - margin, PAD + cols + margin, 8)

    own = pltpu.make_async_copy(
        cells_ref, even_field.at[pl.ds(HALO, rows), pl.ds(PAD, cols), :], in_sems.at[0]
    )
    own.start()
    one = pltpu.make_async_copy(
        one_ref, even_field.at[pl.ds(jnp.where(row_first, rows + HALO, 0), HALO), wide, :], in_sems.at[1]
    )
    one.start()
    two = pltpu.make_async_copy(
        two_ref, even_field.at[pl.ds(jnp.where(row_first, 0, rows + HALO), HALO), wide, :], in_sems.at[2]
    )
    two.start()

    def sides(x, _):
        near = near_ref[pl.ds(x * HALO, HALO), :]
        far = far_ref[pl.ds(x * HALO, HALO), :]
        even_field[HALO + x, PAD - HALO : PAD, :] = jnp.where(col_first, far, near)
        even_field[HALO + x, PAD + cols : PAD + cols + HALO, :] = jnp.where(col_first, near, far)
        return 0

    lax.fori_loop(0, rows, sides, 0)
    own.wait()
    one.wait()
    two.wait()

    def stiffness(x, _):
        stiff[x, wide, :] = jnp.broadcast_to(
            even_field[x, wide, vectors : vectors + 1] * (2.0 / HALF), (cols + 2 * margin, LANES)
        )
        return 0

    lax.fori_loop(0, rows + 2 * HALO, stiffness, 0)

    def around(ref, x, y, step):
        mid = ref[pl.ds(x - 1, step + 2), pl.ds(y, 8), :]
        left = ref[pl.ds(x, step), pl.ds(y - 1, 8), :]
        right = ref[pl.ds(x, step), pl.ds(y + 1, 8), :]
        return ((mid[:-2] + mid[2:]) + (left + right)) - 4.0 * mid[1:-1]

    def sweep(low, high, step, ys, work):
        def chunk(i, _):
            for y in ys:
                work(low + i * step, y)
            return 0

        lax.fori_loop(0, (high - low) // step, chunk, 0)

    step = 4

    def clear(field):
        blank = jnp.zeros((8, LANES), F32)

        def rows_at(start):
            for x in range(HALO):
                field[start + x, wide, :] = jnp.zeros((cols + 2 * margin, LANES), F32)

        def cols_at(start):
            def one_row(x, _):
                field[x, start : start + 8, :] = blank
                return 0

            lax.fori_loop(0, rows + 2 * HALO, one_row, 0)

        pl.when(row == 0)(lambda: rows_at(0))
        pl.when(row == row_count - 1)(lambda: rows_at(HALO + rows))
        pl.when(col == 0)(lambda: cols_at(PAD - 8))
        pl.when(col == col_count - 1)(lambda: cols_at(PAD + cols))

    lead = (CENTER - SHIFT) / HALF
    for k in range(DEGREE):
        current, following = (even_field, odd_field) if k % 2 == 0 else (odd_field, even_field)
        low, high = 1 + 2 * k, rows + 2 * HALO - 1 - 2 * k

        def first_half(x, y):
            inner[pl.ds(x, step), pl.ds(y, 8), :] = stiff[pl.ds(x, step), pl.ds(y, 8), :] * around(
                current, x, y, step
            )

        def second_half(x, y):
            image = around(inner, x, y, step)
            here = current[pl.ds(x, step), pl.ds(y, 8), :]
            if k == 0:
                result = lead * here - 0.5 * image
            else:
                before = following[pl.ds(x, step), pl.ds(y, 8), :]
                result = (2.0 * lead * here - before) - image
            following[pl.ds(x, step), pl.ds(y, 8), :] = result

        sweep(low, high, step, tiles, first_half)
        sweep(low, high, step, tiles, second_half)
        clear(following)

    final, other = (even_field, odd_field) if DEGREE % 2 == 0 else (odd_field, even_field)

    def last_half(x, y):
        bend = around(final, x, y, step)
        inner[pl.ds(x, step), pl.ds(y, 8), :] = bend
        other[pl.ds(x, step), pl.ds(y, 8), :] = stiff[pl.ds(x, step), pl.ds(y, 8), :] * bend

    sweep(HALO, HALO + rows, step, range(PAD, PAD + cols, 8), last_half)

    sums[...] = jnp.zeros_like(sums)

    def product(index, lhs, rhs):
        lhs_high, lhs_low = split(lhs)
        rhs_high, rhs_low = split(rhs)
        sums[index] += jnp.dot(
            jnp.concatenate([lhs_high, lhs_low], axis=0),
            jnp.concatenate([rhs_high, rhs_low], axis=1),
            preferred_element_type=F32,
        )

    mine = pl.ds(PAD, cols)
    group = 4

    def grams(i, _):
        x = i * group
        fields = [final[HALO + x + j, mine, :] for j in range(group)]
        flipped = [f.T[:vectors] for f in fields]
        for j in range(group):
            turned[x + j] = flipped[j]
        product(0, jnp.concatenate(flipped, axis=1), jnp.concatenate(fields, axis=0))
        bends = [inner[HALO + x + j, mine, :] for j in range(group)]
        stressed = [other[HALO + x + j, mine, :].T[:vectors] for j in range(group)]
        product(1, jnp.concatenate(stressed, axis=1), jnp.concatenate(bends, axis=0))
        return 0

    lax.fori_loop(0, rows // group, grams, 0)
    out = pltpu.make_async_copy(turned, turned_ref, out_sem)
    out.start()

    def total(index):
        both = sums[index, :vectors] + sums[index, vectors:]
        return both[:, :LANES] + both[:, LANES:]

    gram, image_gram = total(0), total(1)
    i = lax.broadcasted_iota(jnp.int32, (vectors, LANES), 0)
    j = lax.broadcasted_iota(jnp.int32, (vectors, LANES), 1)
    diagonal = jnp.sum(jnp.where(i == j, image_gram, 0.0), axis=1, keepdims=True)
    packed = jnp.where(j <= i, gram, image_gram)
    sums_ref[...] = jnp.where(j < vectors, packed, jnp.where(j == vectors, diagonal, 0.0))
    out.wait()


def filtered(vectors, cells, near, far, one, two):
    rows, cols, _ = cells.shape
    vmem, hbm = pl.BlockSpec(memory_space=pltpu.VMEM), pl.BlockSpec(memory_space=pl.ANY)
    padded = pltpu.VMEM((rows + 2 * HALO + 2, cols + 2 * PAD, LANES), F32)
    return pl.pallas_call(
        functools.partial(filter_kernel, vectors),
        in_specs=[hbm, vmem, vmem, hbm, hbm],
        out_specs=[hbm, vmem],
        out_shape=[
            jax.ShapeDtypeStruct((rows, vectors, cols), F32),
            jax.ShapeDtypeStruct((vectors, LANES), F32),
        ],
        scratch_shapes=[padded] * 4 + [
            pltpu.VMEM((rows, vectors, cols), F32),
            pltpu.VMEM((2, 2 * vectors, 2 * LANES), F32),
            pltpu.SemaphoreType.DMA((3,)),
            pltpu.SemaphoreType.DMA,
        ],
        compiler_params=pltpu.CompilerParams(vmem_limit_bytes=48 * MIB),
    )(cells, near, far, one, two)


def inverse_factor(gram, vectors):
    lane = lax.broadcasted_iota(jnp.int32, (8, LANES), 1)
    blocks = [gram[8 * b : 8 * b + 8] for b in range(vectors // 8)]
    sub = lax.broadcasted_iota(jnp.int32, (8, LANES), 0)
    for j in range(vectors):
        b, s = j // 8, j % 8
        row = jnp.broadcast_to(blocks[b][s : s + 1, :], (8, LANES))
        pivot = jnp.broadcast_to(row[:, j : j + 1], (8, LANES))
        scaled = jnp.where(lane == j, 1.0, row) / pivot
        for t in range(b, vectors // 8):
            column = jnp.broadcast_to(blocks[t][:, j : j + 1], (8, LANES))
            new = jnp.where(lane == j, 0.0, blocks[t]) - column * scaled
            if t == b:
                own = jnp.where(lane == j, 1.0, row) * lax.rsqrt(pivot)
                new = jnp.where(sub > s, new, jnp.where(sub == s, own, blocks[t]))
            blocks[t] = new
    full = jnp.concatenate(blocks, axis=0)
    i = lax.broadcasted_iota(jnp.int32, (vectors, LANES), 0)
    j = lax.broadcasted_iota(jnp.int32, (vectors, LANES), 1)
    return jnp.where(j <= i, full, 0.0)


def finish_kernel(scale, sums_ref, turned_ref, basis_ref, projected_ref, turned, basis, in_sem, out_sems):
    rows, vectors, cols = turned_ref.shape
    fetch = pltpu.make_async_copy(turned_ref, turned, in_sem)
    fetch.start()
    packed = sums_ref[...]
    i = lax.broadcasted_iota(jnp.int32, (vectors, LANES), 0)
    j = lax.broadcasted_iota(jnp.int32, (vectors, LANES), 1)
    square = jnp.concatenate([packed, jnp.zeros((LANES - vectors, LANES), F32)], axis=0)
    flipped = square.T[:vectors]
    gram = jnp.where(j <= i, packed, flipped)
    image_gram = jnp.where(j > i, packed, jnp.where(j < i, flipped, packed[:, vectors : vectors + 1]))
    image_gram = jnp.where(j < vectors, image_gram, 0.0)
    inverse = inverse_factor(jnp.where(j < vectors, gram, 0.0), vectors)
    middle = jnp.dot(
        inverse[:, :vectors], image_gram, preferred_element_type=F32, precision=lax.Precision.HIGHEST
    )
    sandwich = lax.dot_general(
        middle, inverse, (((1,), (1,)), ((), ())), preferred_element_type=F32, precision=lax.Precision.HIGHEST
    )
    k = lax.broadcasted_iota(jnp.int32, (vectors, vectors), 0)
    m = lax.broadcasted_iota(jnp.int32, (vectors, vectors), 1)
    projected_ref[...] = sandwich * (HALF / (2.0 * TOP)) + jnp.where(k == m, SHIFT / TOP, 0.0)

    high, low = split(inverse[:, :vectors] * scale)
    fetch.wait()
    group = 8
    for x in range(0, rows, group):
        for g in range(0, group, 2):
            pair = jnp.concatenate([turned[x + g], turned[x + g + 1]], axis=1)
            pair_high, pair_low = split(pair)
            result = jnp.dot(high, pair_low, preferred_element_type=F32)
            result += jnp.dot(low, pair_high, preferred_element_type=F32)
            result += jnp.dot(high, pair_high, preferred_element_type=F32)
            basis[:, x + g, :] = result[:, :cols]
            basis[:, x + g + 1, :] = result[:, cols:]
        pltpu.make_async_copy(
            basis.at[:, pl.ds(x, group), :], basis_ref.at[:, pl.ds(x, group), :], out_sems.at[x // group]
        ).start()
    for x in range(0, rows, group):
        pltpu.make_async_copy(
            basis.at[:, pl.ds(x, group), :], basis_ref.at[:, pl.ds(x, group), :], out_sems.at[x // group]
        ).wait()


def finish(sums, turned, scale):
    rows, vectors, cols = turned.shape
    vmem, hbm = pl.BlockSpec(memory_space=pltpu.VMEM), pl.BlockSpec(memory_space=pl.ANY)
    return pl.pallas_call(
        functools.partial(finish_kernel, scale),
        in_specs=[vmem, hbm],
        out_specs=[hbm, vmem],
        out_shape=[
            jax.ShapeDtypeStruct((vectors, rows, cols), F32),
            jax.ShapeDtypeStruct((vectors, vectors), F32),
        ],
        scratch_shapes=[
            pltpu.VMEM((rows, vectors, cols), F32),
            pltpu.VMEM((vectors, rows, cols), F32),
            pltpu.SemaphoreType.DMA,
            pltpu.SemaphoreType.DMA((rows // 8,)),
        ],
        compiler_params=pltpu.CompilerParams(vmem_limit_bytes=32 * MIB),
    )(sums, turned)


def pairs(count, start):
    found = []
    for i in range(start, count - 1, 2):
        found += [(i, i + 1), (i + 1, i)]
    return found


def all_sum(values, axes):
    count = 1
    for axis in axes:
        count *= lax.axis_size(axis)
    if count & (count - 1):
        return lax.psum(values, axes)
    step = 1
    while step < count:
        values = values + lax.ppermute(values, axes, [(i, i ^ step) for i in range(count)])
        step *= 2
    return values


def body(start_block, stiffness):
    vectors, rows, cols = start_block.shape
    row_count, col_count = lax.axis_size("row"), lax.axis_size("col")
    cells, near, far = turn(start_block, stiffness)
    near = lax.ppermute(near, "col", pairs(col_count, 0))
    far = lax.ppermute(far, "col", pairs(col_count, 1))
    one, two = edges(cells, near, far)
    one = lax.ppermute(one, "row", pairs(row_count, 0))
    two = lax.ppermute(two, "row", pairs(row_count, 1))
    turned, sums = filtered(vectors, cells, near, far, one, two)
    sums = all_sum(sums, ("row", "col"))
    scale = float(rows * row_count * cols * col_count) ** 0.5
    return tuple(finish(sums, turned, scale))


def solution(mesh):
    in_specs = (P(None, "row", "col"), P("row", "col"))
    out_specs = (P(None, "row", "col"), P())
    return jax.shard_map(body, mesh=mesh, in_specs=in_specs, out_specs=out_specs, check_vma=False)
```

```python
import functools
import jax
import jax.numpy as jnp
from jax import lax
from jax.experimental import pallas as pl
from jax.experimental.pallas import tpu as pltpu
from jax.sharding import PartitionSpec as P

DEGREE = 4
TOP = 129.0
CUT = 16.0
SHIFT = 1.0
CENTER = (TOP + CUT) / 2.0
HALF = (TOP - CUT) / 2.0
LEAD = (CENTER - SHIFT) / HALF
HALO = 2 * DEGREE + 1
MARGIN = HALO - 1
LANES = 128
PAD = 16
GROUP = 4
F32 = jnp.float32
BF16 = jnp.bfloat16
MIB = 2**20
VMEM = pl.BlockSpec(memory_space=pltpu.VMEM)
HBM = pl.BlockSpec(memory_space=pl.ANY)


def split(values):
    high = values.astype(BF16)
    low = (values - high.astype(F32)).astype(BF16)
    return high, low


def even(index):
    return lax.rem(index, 2) == 0


def loop(count, work):
    def one(i, carry):
        work(i)
        return carry

    lax.fori_loop(0, count, one, 0)


def params(limit):
    return pltpu.CompilerParams(vmem_limit_bytes=limit * MIB)


def padded(rows, cols):
    return jax.ShapeDtypeStruct((rows + 2 * HALO, cols + 2 * PAD, LANES), F32)


def lanes_up(block, stiff):
    vectors, cols = block.shape
    fill = jnp.zeros((LANES - vectors - 8, cols), F32)
    return jnp.concatenate([block, jnp.broadcast_to(stiff, (8, cols)), fill], axis=0).T


def spread_stiffness(row):
    return jnp.broadcast_to(row * (2.0 / HALF), (LANES, row.shape[1])).T


def turn_kernel(block_ref, stiff_ref, field, near, far, one, two, held, sems):
    chunks, vectors, step, cols = held.shape
    rows = chunks * step
    col_first, row_first = even(lax.axis_index("col")), even(lax.axis_index("row"))
    copies = [
        pltpu.make_async_copy(block_ref.at[:, pl.ds(i * step, step), :], held.at[i], sems.at[i])
        for i in range(chunks)
    ]
    for copy in copies:
        copy.start()

    def chunk(i):
        pltpu.make_async_copy(block_ref.at[:, pl.ds(i * step, step), :], held.at[i], sems.at[i]).wait()
        for r in range(step):
            x = i * step + r
            turned = lanes_up(held[i, :, r, :], stiff_ref[pl.ds(x, 1), :])
            field[HALO + x, PAD : PAD + cols, :] = turned
            head, tail = turned[:HALO], turned[cols - HALO :]
            near[pl.ds(x * HALO, HALO), :] = jnp.where(col_first, tail, head)
            far[pl.ds(x * HALO, HALO), :] = jnp.where(col_first, head, tail)

    loop(chunks, chunk)
    for r in range(HALO):
        end = rows - HALO + r
        head = held[r // step, :, r % step, :]
        tail = held[end // step, :, end % step, :]
        one[r * vectors : (r + 1) * vectors, :] = jnp.where(row_first, tail, head)
        two[r * vectors : (r + 1) * vectors, :] = jnp.where(row_first, head, tail)


def turn(block, stiffness):
    vectors, rows, cols = block.shape
    side = jax.ShapeDtypeStruct((rows * HALO, LANES), F32)
    end = jax.ShapeDtypeStruct((HALO * vectors, cols), F32)
    step = 8
    return pl.pallas_call(
        turn_kernel,
        in_specs=[HBM, VMEM],
        out_specs=[VMEM] * 5,
        out_shape=[padded(rows, cols), side, side, end, end],
        scratch_shapes=[
            pltpu.VMEM((rows // step, vectors, step, cols), F32),
            pltpu.SemaphoreType.DMA((rows // step,)),
        ],
        compiler_params=params(24),
        cost_estimate=pl.CostEstimate(flops=0, bytes_accessed=4 * vectors * rows * cols * 2, transcendentals=0),
    )(block, stiffness)


def stiff_kernel(stiff_ref, field, stiff):
    rows, cols = stiff_ref.shape
    step = 8

    def some(i):
        for r in range(step):
            x = i * step + r
            stiff[HALO + x, PAD : PAD + cols, :] = spread_stiffness(stiff_ref[pl.ds(x, 1), :])

    loop(rows // step, some)


def own_stiffness(stiffness, field):
    rows, cols = stiffness.shape
    return pl.pallas_call(
        stiff_kernel,
        in_specs=[VMEM, HBM],
        out_specs=VMEM,
        out_shape=padded(rows, cols),
        compiler_params=params(16),
        cost_estimate=pl.CostEstimate(flops=0, bytes_accessed=4 * LANES * rows * cols, transcendentals=0),
    )(stiffness, field)


def corner_kernel(vectors, field_in, stiff_in, stiff_ref, near, far, field, stiff, one, two):
    rows, cols = stiff_ref.shape
    col_first, row_first = even(lax.axis_index("col")), even(lax.axis_index("row"))
    step = 8
    ends = (PAD - MARGIN, PAD + cols)

    def some(i):
        for r in range(step):
            x = i * step + r
            a, b = near[pl.ds(x * HALO, HALO), :], far[pl.ds(x * HALO, HALO), :]
            field[HALO + x, PAD - HALO : PAD, :] = jnp.where(col_first, b, a)
            field[HALO + x, PAD + cols : PAD + cols + HALO, :] = jnp.where(col_first, a, b)
        for r in range(step):
            x = HALO + i * step + r
            for y in ends:
                lane = field[x, y : y + MARGIN, vectors : vectors + 1] * (2.0 / HALF)
                stiff[x, y : y + MARGIN, :] = jnp.broadcast_to(lane, (MARGIN, LANES))

    loop(rows // step, some)
    last = rows - HALO
    for out, start in ((one, jnp.where(row_first, last, 0)), (two, jnp.where(row_first, 0, last))):
        for r in range(HALO):
            for e, y in enumerate(ends):
                out[(2 * r + e) * MARGIN : (2 * r + e + 1) * MARGIN, :] = field[HALO + start + r, y : y + MARGIN, :]
        base = 2 * HALO * MARGIN
        out[base:, :] = jnp.zeros((out.shape[0] - base, LANES), F32)
    base = 2 * HALO * MARGIN
    head, tail = stiff_ref[:HALO, :], stiff_ref[last:, :]
    one[base : base + HALO, :] = jnp.where(row_first, tail, head)
    two[base : base + HALO, :] = jnp.where(row_first, head, tail)


def corners(vectors, field, stiff, stiffness, near, far):
    rows, cols = stiffness.shape
    corner = jax.ShapeDtypeStruct((2 * HALO * MARGIN + 16, LANES), F32)
    return pl.pallas_call(
        functools.partial(corner_kernel, vectors),
        in_specs=[VMEM] * 5,
        out_specs=[VMEM] * 4,
        out_shape=[padded(rows, cols), padded(rows, cols), corner, corner],
        input_output_aliases={0: 0, 1: 1},
        compiler_params=params(16),
    )(field, stiff, stiffness, near, far)


def around(ref, x, y, step):
    mid = ref[pl.ds(x - 1, step + 2), pl.ds(y, 8), :]
    left = ref[pl.ds(x, step), pl.ds(y - 1, 8), :]
    right = ref[pl.ds(x, step), pl.ds(y + 1, 8), :]
    return ((mid[:-2] + mid[2:]) + (left + right)) - 4.0 * mid[1:-1]


def bend(field, stiff, inner, x, y, step):
    at = (pl.ds(x, step), pl.ds(y, 8))
    inner[*at, :] = stiff[*at, :] * around(field, x, y, step)


def advance(k, current, inner, following, x, y, step):
    at = (pl.ds(x, step), pl.ds(y, 8))
    image = around(inner, x, y, step)
    here = current[*at, :]
    if k == 0:
        following[*at, :] = LEAD * here - 0.5 * image
    else:
        following[*at, :] = (2.0 * LEAD * here - following[*at, :]) - image


def root_bend(field, stiff, inner, x, y, step):
    at = (pl.ds(x, step), pl.ds(y, 8))
    weight = stiff[*at, :]
    inner[*at, :] = weight * lax.rsqrt(weight) * around(field, x, y, step)


def sweep(low, high, ys, work):
    step = 4
    whole = (high - low) // step

    def chunk(i):
        for y in ys:
            work(low + i * step, y, step)

    loop(whole, chunk)
    rest = (high - low) - whole * step
    if rest:
        for y in ys:
            work(high - rest, y, rest)


def clear_cols(field, low, high, cols):
    col, count = lax.axis_index("col"), lax.axis_size("col")

    def at(start):
        field[low:high, start : start + MARGIN, :] = jnp.zeros((high - low, MARGIN, LANES), F32)

    pl.when(col == 0)(lambda: at(PAD - MARGIN))
    pl.when(col == count - 1)(lambda: at(PAD + cols))


def clear_rows(field, rows, cols):
    row, count = lax.axis_index("row"), lax.axis_size("row")

    def at(start):
        wide = cols + 2 * MARGIN
        for x in range(start, start + HALO):
            field[x, PAD - MARGIN : PAD + cols + MARGIN, :] = jnp.zeros((wide, LANES), F32)

    pl.when(row == 0)(lambda: at(0))
    pl.when(row == count - 1)(lambda: at(HALO + rows))


def prepare(slot, x, j, vectors, cols, field, inner, turned, lhs):
    cells = field[HALO + x, PAD : PAD + cols, :].T[:vectors]
    turned[x] = cells
    lhs[slot, 0, :, j * cols : (j + 1) * cols] = cells.astype(BF16)
    lhs[slot, 1, :, j * cols : (j + 1) * cols] = inner[HALO + x, PAD : PAD + cols, :].astype(BF16).T[:vectors]


def multiply(slot, xs, cols, field, inner, lhs, sums):
    for which, ref in enumerate((field, inner)):
        cells = jnp.concatenate([ref[HALO + x, PAD : PAD + cols, :] for x in xs], axis=0)
        high, low = split(cells)
        sums[which] += jnp.dot(
            lhs[slot, which], jnp.concatenate([high, low], axis=1), preferred_element_type=F32
        )


def middle_kernel(vectors, rows, cols, field_in, stiff, field, odd, inner, turned, sums, lhs):
    tiles = range(PAD - MARGIN, PAD + cols + MARGIN, 8)
    terms = (field, odd)
    for k in range(DEGREE):
        current, following = terms[k % 2], terms[(k + 1) % 2]
        low, high = HALO + 1 + 2 * k, HALO + rows - 1 - 2 * k
        sweep(low, high, tiles, functools.partial(bend, current, stiff, inner))
        sweep(low + 1, high - 1, tiles, functools.partial(advance, k, current, inner, following))
        clear_cols(following, low + 1, high - 1, cols)
    low, high = HALO, rows - HALO
    own = range(PAD, PAD + cols, 8)
    sweep(HALO + low, HALO + high, own, functools.partial(root_bend, terms[DEGREE % 2], stiff, inner))

    first = low + 1
    groups = (high - 1 - first) // GROUP
    sums[...] = jnp.zeros_like(sums)
    final = terms[DEGREE % 2]

    def rows_of(g):
        return [first + g * GROUP + j for j in range(GROUP)]

    def ready(g, slot):
        for j, x in enumerate(rows_of(g)):
            prepare(slot, x, j, vectors, cols, final, inner, turned, lhs)

    ready(0, 0)

    def one(g):
        slot = lax.rem(g, 2)
        multiply(slot, rows_of(g), cols, final, inner, lhs, sums)
        ready(g + 1, 1 - slot)

    loop(groups - 1, one)
    multiply((groups - 1) % 2, rows_of(groups - 1), cols, final, inner, lhs, sums)


def middle(vectors, rows, cols, field, stiff):
    big = padded(rows, cols)
    return pl.pallas_call(
        functools.partial(middle_kernel, vectors, rows, cols),
        in_specs=[VMEM] * 2,
        out_specs=[VMEM] * 5,
        out_shape=[
            big,
            big,
            big,
            jax.ShapeDtypeStruct((rows, vectors, cols), F32),
            jax.ShapeDtypeStruct((2, vectors, 2 * LANES), F32),
        ],
        input_output_aliases={0: 0},
        scratch_shapes=[pltpu.VMEM((2, 2, vectors, GROUP * cols), BF16)],
        compiler_params=params(24),
        cost_estimate=pl.CostEstimate(flops=10**10, bytes_accessed=40 * MIB, transcendentals=0),
    )(field, stiff)


def ends_kernel(vectors, rows, cols, field_in, odd_in, inner_in, stiff_in, turned_in, sums_in,
                one, two, corner_one, corner_two, field, odd, inner, stiff, turned, packed, sums, lhs):
    row_first = even(lax.axis_index("row"))
    base = 2 * HALO * MARGIN

    def fill(start, block, corner):
        for r in range(HALO):
            x = start + r
            weight = corner[base + r : base + r + 1, :]
            field[x, PAD : PAD + cols, :] = lanes_up(block[r * vectors : (r + 1) * vectors, :], weight)
            stiff[x, PAD : PAD + cols, :] = spread_stiffness(weight)
            for e, y in enumerate((PAD - MARGIN, PAD + cols)):
                piece = corner[(2 * r + e) * MARGIN : (2 * r + e + 1) * MARGIN, :]
                field[x, y : y + MARGIN, :] = piece
                stiff[x, y : y + MARGIN, :] = jnp.broadcast_to(
                    piece[:, vectors : vectors + 1] * (2.0 / HALF), (MARGIN, LANES)
                )

    fill(jnp.where(row_first, HALO + rows, 0), one, corner_one)
    fill(jnp.where(row_first, 0, HALO + rows), two, corner_two)

    def both(low, high, start, stop, work):
        tops = ((low, 4), (low + 4, high - low - 4))
        flip = rows + 2 * HALO
        spans = tops + tuple((flip - x - n, n) for x, n in tops)
        wide = 2

        def some(i):
            for u in range(wide):
                y = pl.multiple_of(start + (i * wide + u) * 8, 8)
                for x, n in spans:
                    work(x, y, n)

        loop((stop - start) // (8 * wide), some)

    terms = (field, odd)
    for k in range(DEGREE):
        current, following = terms[k % 2], terms[(k + 1) % 2]
        low = 1 + 2 * k
        span = (PAD - MARGIN, PAD + cols + MARGIN)
        both(low, low + HALO, *span, functools.partial(bend, current, stiff, inner))
        both(low + 1, low + 1 + HALO, *span, functools.partial(advance, k, current, inner, following))
        clear_cols(following, low + 1, low + 1 + HALO, cols)
        clear_cols(following, rows + 2 * HALO - low - 1 - HALO, rows + 2 * HALO - low - 1, cols)
        clear_rows(following, rows, cols)
    final = terms[DEGREE % 2]
    both(HALO, 2 * HALO, PAD, PAD + cols, functools.partial(root_bend, final, stiff, inner))

    sums[...] = sums_in[...]
    xs = list(range(HALO + 1)) + list(range(rows - HALO - 1, rows))
    for g in range(0, len(xs), GROUP):
        for j, x in enumerate(xs[g : g + GROUP]):
            prepare(g // GROUP % 2, x, j, vectors, cols, final, inner, turned, lhs)
        multiply(g // GROUP % 2, xs[g : g + GROUP], cols, final, inner, lhs, sums)

    def total(which):
        high, low = sums[which, :, :LANES], sums[which, :, LANES:]
        square = jnp.concatenate([low, jnp.zeros((LANES - vectors, LANES), F32)], axis=0)
        return high + (low + square.T[:vectors])

    gram, image_gram = total(0), total(1)
    i = lax.broadcasted_iota(jnp.int32, (vectors, LANES), 0)
    j = lax.broadcasted_iota(jnp.int32, (vectors, LANES), 1)
    diagonal = jnp.sum(jnp.where(i == j, image_gram, 0.0), axis=1, keepdims=True)
    both_grams = jnp.where(j <= i, gram, image_gram)
    packed[...] = jnp.where(j < vectors, both_grams, jnp.where(j == vectors, diagonal, 0.0))


def ends(vectors, rows, cols, field, odd, inner, stiff, turned, sums, one, two, corner_one, corner_two):
    big = padded(rows, cols)
    return pl.pallas_call(
        functools.partial(ends_kernel, vectors, rows, cols),
        in_specs=[VMEM] * 10,
        out_specs=[VMEM] * 6,
        out_shape=[
            big,
            big,
            big,
            big,
            jax.ShapeDtypeStruct((rows, vectors, cols), F32),
            jax.ShapeDtypeStruct((vectors, LANES), F32),
        ],
        input_output_aliases={0: 0, 1: 1, 2: 2, 3: 3, 4: 4},
        scratch_shapes=[
            pltpu.VMEM((2, vectors, 2 * LANES), F32),
            pltpu.VMEM((2, 2, vectors, GROUP * cols), BF16),
        ],
        compiler_params=params(24),
    )(field, odd, inner, stiff, turned, sums, one, two, corner_one, corner_two)[4:]


def inverse_factor(gram, vectors):
    lane = lax.broadcasted_iota(jnp.int32, (8, LANES), 1)
    sub = lax.broadcasted_iota(jnp.int32, (8, LANES), 0)
    count = vectors // 8
    blocks = [gram[8 * b : 8 * b + 8] for b in range(count)]

    def spread(values, j):
        return jnp.broadcast_to(values[:, j : j + 1], (8, LANES))

    done = []
    for b in range(count):
        base = 8 * b
        own = (lane >= base) & (lane < base + 8)
        raw = [jnp.broadcast_to(blocks[b][s : s + 1], (8, LANES)) for s in range(8)]
        pivots = [[spread(raw[s], base + k) if k >= s else None for k in range(8)] for s in range(8)]
        below = {t: [spread(blocks[t], base + k) for k in range(8)] for t in range(b + 1, count)}
        rows = [jnp.where(own, jnp.where(lane == base + s, 1.0, 0.0), raw[s]) for s in range(8)]
        for t in range(b + 1, count):
            blocks[t] = jnp.where(own, 0.0, blocks[t])
        finished = jnp.zeros((8, LANES), F32)
        for s in range(8):
            inverse = 1.0 / pivots[s][s]
            for i in range(s + 1, 8):
                m = pivots[s][i] * inverse
                for k in range(i, 8):
                    pivots[i][k] = pivots[i][k] - m * pivots[s][k]
                rows[i] = rows[i] - m * rows[s]
            finished = jnp.where(sub == s, rows[s] * lax.rsqrt(pivots[s][s]), finished)
            for t in range(b + 1, count):
                q = below[t][s] * inverse
                for k in range(s + 1, 8):
                    below[t][k] = below[t][k] - q * pivots[s][k]
                blocks[t] = blocks[t] - q * rows[s]
        done.append(finished)
    full = jnp.concatenate(done, axis=0)
    i = lax.broadcasted_iota(jnp.int32, (vectors, LANES), 0)
    j = lax.broadcasted_iota(jnp.int32, (vectors, LANES), 1)
    return jnp.where(j <= i, full, 0.0)


def finish_kernel(scale, sums_ref, turned, basis_ref, projected_ref, basis, out_sems):
    rows, vectors, cols = turned.shape
    packed = sums_ref[...]
    i = lax.broadcasted_iota(jnp.int32, (vectors, LANES), 0)
    j = lax.broadcasted_iota(jnp.int32, (vectors, LANES), 1)
    square = jnp.concatenate([packed, jnp.zeros((LANES - vectors, LANES), F32)], axis=0)
    flipped = square.T[:vectors]
    gram = jnp.where(j <= i, packed, flipped)
    inverse = inverse_factor(jnp.where(j < vectors, gram, 0.0), vectors)

    high, low = split(inverse[:, :vectors] * scale)
    group = 8
    copies = []
    for x in range(0, rows, group):
        for g in range(0, group, 2):
            pair = jnp.concatenate([turned[x + g], turned[x + g + 1]], axis=1)
            pair_high, pair_low = split(pair)
            result = jnp.dot(high, pair_low, preferred_element_type=F32)
            result += jnp.dot(low, pair_high, preferred_element_type=F32)
            result += jnp.dot(high, pair_high, preferred_element_type=F32)
            basis[:, x + g, :] = result[:, :cols]
            basis[:, x + g + 1, :] = result[:, cols:]
        copies.append(
            pltpu.make_async_copy(
                basis.at[:, pl.ds(x, group), :], basis_ref.at[:, pl.ds(x, group), :], out_sems.at[x // group]
            )
        )
        copies[-1].start()

    image_gram = jnp.where(j > i, packed, jnp.where(j < i, flipped, packed[:, vectors : vectors + 1]))
    image_gram = jnp.where(j < vectors, image_gram, 0.0)
    half = jnp.dot(
        inverse[:, :vectors], image_gram, preferred_element_type=F32, precision=lax.Precision.HIGHEST
    )
    sandwich = lax.dot_general(
        half, inverse, (((1,), (1,)), ((), ())), preferred_element_type=F32, precision=lax.Precision.HIGHEST
    )
    k = lax.broadcasted_iota(jnp.int32, (vectors, vectors), 0)
    m = lax.broadcasted_iota(jnp.int32, (vectors, vectors), 1)
    projected_ref[...] = sandwich * (HALF / (2.0 * TOP)) + jnp.where(k == m, SHIFT / TOP, 0.0)
    for copy in copies:
        copy.wait()


def finish(sums, turned, scale):
    rows, vectors, cols = turned.shape
    return pl.pallas_call(
        functools.partial(finish_kernel, scale),
        in_specs=[VMEM, VMEM],
        out_specs=[HBM, VMEM],
        out_shape=[
            jax.ShapeDtypeStruct((vectors, rows, cols), F32),
            jax.ShapeDtypeStruct((vectors, vectors), F32),
        ],
        scratch_shapes=[
            pltpu.VMEM((vectors, rows, cols), F32),
            pltpu.SemaphoreType.DMA((rows // 8,)),
        ],
        compiler_params=params(24),
    )(sums, turned)


def pairs(count, start):
    found = []
    for i in range(start, count - 1, 2):
        found += [(i, i + 1), (i + 1, i)]
    return found


def all_sum(values, axes):
    count = 1
    for axis in axes:
        count *= lax.axis_size(axis)
    if count & (count - 1):
        return lax.psum(values, axes)
    step = 1
    while step < count:
        values = values + lax.ppermute(values, axes, [(i, i ^ step) for i in range(count)])
        step *= 2
    return values


def body(start_block, stiffness):
    vectors, rows, cols = start_block.shape
    row_count, col_count = lax.axis_size("row"), lax.axis_size("col")
    field, near, far, one, two = turn(start_block, stiffness)
    near = lax.ppermute(near, "col", pairs(col_count, 0))
    far = lax.ppermute(far, "col", pairs(col_count, 1))
    one = lax.ppermute(one, "row", pairs(row_count, 0))
    two = lax.ppermute(two, "row", pairs(row_count, 1))
    stiff = own_stiffness(stiffness, field)
    field, stiff, corner_one, corner_two = corners(vectors, field, stiff, stiffness, near, far)
    corner_one = lax.ppermute(corner_one, "row", pairs(row_count, 0))
    corner_two = lax.ppermute(corner_two, "row", pairs(row_count, 1))
    field, odd, inner, turned, sums = middle(vectors, rows, cols, field, stiff)
    turned, sums = ends(
        vectors, rows, cols, field, odd, inner, stiff, turned, sums, one, two, corner_one, corner_two
    )
    sums = all_sum(sums, ("row", "col"))
    scale = float(rows * row_count * cols * col_count) ** 0.5
    return tuple(finish(sums, turned, scale))


def solution(mesh):
    in_specs = (P(None, "row", "col"), P("row", "col"))
    out_specs = (P(None, "row", "col"), P())
    return jax.shard_map(body, mesh=mesh, in_specs=in_specs, out_specs=out_specs, check_vma=False)
```

```python
import functools
import jax
import jax.numpy as jnp
from jax import lax
from jax.experimental import pallas as pl
from jax.experimental.pallas import tpu as pltpu
from jax.sharding import PartitionSpec as P

DEGREE = 4
TOP = 129.0
CUT = 16.0
SHIFT = 1.0
CENTER = (TOP + CUT) / 2.0
HALF = (TOP - CUT) / 2.0
LEAD = (CENTER - SHIFT) / HALF
HALO = 2 * DEGREE + 1
MARGIN = HALO - 1
FIRST = 5
EARLY = 1
LANES = 128
PAD = 16
GROUP = 4
F32 = jnp.float32
BF16 = jnp.bfloat16
MIB = 2**20
VMEM = pl.BlockSpec(memory_space=pltpu.VMEM)
HBM = pl.BlockSpec(memory_space=pltpu.HBM)


def split(values):
    high = values.astype(BF16)
    low = (values - high.astype(F32)).astype(BF16)
    return high, low


def even(index):
    return lax.rem(index, 2) == 0


def loop(count, work):
    def one(i, carry):
        work(i)
        return carry

    lax.fori_loop(0, count, one, 0)


def params(limit):
    return pltpu.CompilerParams(vmem_limit_bytes=limit * MIB)


def padded(rows, cols):
    return jax.ShapeDtypeStruct((rows + 2 * HALO, cols + 2 * PAD, LANES), F32)


def lanes_up(block, stiff):
    vectors, cols = block.shape
    fill = jnp.zeros((LANES - vectors - 8, cols), F32)
    return jnp.concatenate([block, jnp.broadcast_to(stiff, (8, cols)), fill], axis=0).T


def spread_stiffness(row):
    return jnp.broadcast_to(row * (2.0 / HALF), (LANES, row.shape[1])).T


def turn_kernel(block_ref, stiff_ref, field, near, far, one, two, rest, stiff, held, sems, slab_sems):
    chunks, vectors, step, cols = held.shape
    rows = chunks * step
    col_first, row_first = even(lax.axis_index("col")), even(lax.axis_index("row"))
    stiff_copy = pltpu.make_async_copy(stiff_ref, stiff, sems.at[chunks])
    copies = [
        pltpu.make_async_copy(block_ref.at[:, pl.ds(i * step, step), :], held.at[i], sems.at[i])
        for i in range(chunks)
    ]
    slab_copies = []
    for which, start in enumerate(
        (jnp.where(row_first, rows - HALO, 0), jnp.where(row_first, 0, rows - HALO))
    ):
        for r in range(HALO):
            out, at = (one, r) if which == 0 else (two, r) if r < FIRST else (rest, r - FIRST)
            slab_copies.append(
                pltpu.make_async_copy(
                    block_ref.at[:, start + r, :], out.at[pl.ds(at * vectors, vectors), :], slab_sems.at[which, r]
                )
            )
    for copy in [stiff_copy] + copies + slab_copies:
        copy.start()
    stiff_copy.wait()
    for i in range(chunks):
        copies[i].wait()
        for r in range(step):
            x = i * step + r
            turned = lanes_up(held[i, :, r, :], stiff[x : x + 1, :])
            field[HALO + x, PAD : PAD + cols, :] = turned
            head, tail = turned[:HALO], turned[cols - HALO :]
            near[x * HALO : (x + 1) * HALO, :] = jnp.where(col_first, tail, head)
            far[x * HALO : (x + 1) * HALO, :] = jnp.where(col_first, head, tail)
    for copy in slab_copies:
        copy.wait()


def turn(block, stiffness):
    vectors, rows, cols = block.shape
    side = jax.ShapeDtypeStruct((rows * HALO, LANES), F32)

    def slab(count):
        return jax.ShapeDtypeStruct((count * vectors, cols), F32)

    step = 16
    return pl.pallas_call(
        turn_kernel,
        in_specs=[HBM] * 2,
        out_specs=[VMEM] * 7,
        out_shape=[
            padded(rows, cols),
            side,
            side,
            slab(HALO),
            slab(FIRST),
            slab(HALO - FIRST),
            jax.ShapeDtypeStruct(stiffness.shape, F32),
        ],
        scratch_shapes=[
            pltpu.VMEM((rows // step, vectors, step, cols), F32),
            pltpu.SemaphoreType.DMA((rows // step + 1,)),
            pltpu.SemaphoreType.DMA((2, HALO)),
        ],
        compiler_params=params(8),
        cost_estimate=pl.CostEstimate(flops=0, bytes_accessed=4 * vectors * rows * cols * 2, transcendentals=0),
    )(
        pltpu.with_memory_space_constraint(block, pltpu.HBM),
        pltpu.with_memory_space_constraint(stiffness, pltpu.HBM),
    )


def corner_kernel(vectors, field_in, stiff_in, stiff_ref, near, far, rest, field, stiff, one, whole):
    rows, cols = stiff_ref.shape
    col_first, row_first = even(lax.axis_index("col")), even(lax.axis_index("row"))
    step = 8
    ends = (PAD - MARGIN, PAD + cols)

    def some(i):
        for r in range(step):
            x = i * step + r
            a, b = near[pl.ds(x * HALO, HALO), :], far[pl.ds(x * HALO, HALO), :]
            field[HALO + x, PAD - HALO : PAD, :] = jnp.where(col_first, b, a)
            field[HALO + x, PAD + cols : PAD + cols + HALO, :] = jnp.where(col_first, a, b)
        for r in range(step):
            x = HALO + i * step + r
            for y in ends:
                lane = field[x, y : y + MARGIN, vectors : vectors + 1] * (2.0 / HALF)
                stiff[x, y : y + MARGIN, :] = jnp.broadcast_to(lane, (MARGIN, LANES))

    loop(rows // step, some)
    last = rows - HALO
    size = rest.shape[0]
    whole[:size, :] = rest[...]
    two = whole.at[size:, :]
    for out, start in ((one, jnp.where(row_first, last, 0)), (two, jnp.where(row_first, 0, last))):
        for r in range(HALO):
            for e, y in enumerate(ends):
                out[(2 * r + e) * MARGIN : (2 * r + e + 1) * MARGIN, :] = field[HALO + start + r, y : y + MARGIN, :]
        base = 2 * HALO * MARGIN
        out[base:, :] = jnp.zeros((out.shape[0] - base, LANES), F32)
    base = 2 * HALO * MARGIN
    head, tail = stiff_ref[:HALO, :], stiff_ref[last:, :]
    one[base : base + HALO, :] = jnp.where(row_first, tail, head)
    two[base : base + HALO, :] = jnp.where(row_first, head, tail)


def corners(vectors, field, stiff, stiffness, near, far, rest):
    rows, cols = stiffness.shape
    corner = jax.ShapeDtypeStruct((2 * HALO * MARGIN + 16, LANES), F32)
    whole = jax.ShapeDtypeStruct((rest.shape[0] + corner.shape[0], LANES), F32)
    return pl.pallas_call(
        functools.partial(corner_kernel, vectors),
        in_specs=[VMEM] * 6,
        out_specs=[VMEM] * 4,
        out_shape=[padded(rows, cols), padded(rows, cols), corner, whole],
        input_output_aliases={0: 0, 1: 1},
        compiler_params=params(4),
        cost_estimate=pl.CostEstimate(flops=0, bytes_accessed=0, transcendentals=0),
    )(field, stiff, stiffness, near, far, rest)


def around(ref, x, y, step):
    mid = ref[pl.ds(x - 1, step + 2), pl.ds(y, 8), :]
    left = ref[pl.ds(x, step), pl.ds(y - 1, 8), :]
    right = ref[pl.ds(x, step), pl.ds(y + 1, 8), :]
    return ((mid[:-2] + mid[2:]) + (left + right)) - 4.0 * mid[1:-1]


def bend(field, stiff, inner, x, y, step):
    at = (pl.ds(x, step), pl.ds(y, 8))
    inner[*at, :] = stiff[*at, :] * around(field, x, y, step)


def advance(k, current, inner, following, x, y, step):
    at = (pl.ds(x, step), pl.ds(y, 8))
    image = around(inner, x, y, step)
    here = current[*at, :]
    if k == 0:
        following[*at, :] = LEAD * here - 0.5 * image
    else:
        following[*at, :] = (2.0 * LEAD * here - following[*at, :]) - image


def root_bend(field, stiff, inner, x, y, step):
    at = (pl.ds(x, step), pl.ds(y, 8))
    weight = stiff[*at, :]
    inner[*at, :] = weight * lax.rsqrt(weight) * around(field, x, y, step)


def sweep(low, high, ys, work):
    step, unroll = 4, 4

    def trip(i):
        for u in range(unroll):
            for y in ys:
                work(low + (i * unroll + u) * step, y, step)

    trips = (high - low) // (step * unroll)
    loop(trips, trip)
    for x in range(low + trips * unroll * step, high, step):
        for y in ys:
            work(x, y, min(step, high - x))


def clear_cols(field, low, high, cols):
    col, count = lax.axis_index("col"), lax.axis_size("col")

    def at(start):
        field[low:high, start : start + MARGIN, :] = jnp.zeros((high - low, MARGIN, LANES), F32)

    pl.when(col == 0)(lambda: at(PAD - MARGIN))
    pl.when(col == count - 1)(lambda: at(PAD + cols))


def clear_rows(field, rows, cols):
    row, count = lax.axis_index("row"), lax.axis_size("row")

    def at(start):
        wide = cols + 2 * MARGIN
        for x in range(start, start + HALO):
            field[x, PAD - MARGIN : PAD + cols + MARGIN, :] = jnp.zeros((wide, LANES), F32)

    pl.when(row == 0)(lambda: at(0))
    pl.when(row == count - 1)(lambda: at(HALO + rows))


def tiles_of(cols, inset):
    return range(PAD - MARGIN + 8 * inset, PAD + cols + MARGIN - 8 * inset, 8)


def operator(k, rows, bends, advances, field, odd, inner, stiff):
    current, following = ((field, odd), (odd, field))[k % 2]
    low, high = HALO + 1 + 2 * k, HALO + rows - 1 - 2 * k
    sweep(low, high, bends, functools.partial(bend, current, stiff, inner))
    sweep(low + 1, high - 1, advances, functools.partial(advance, k, current, inner, following))


def early_kernel(field_in, stiff_ref, field, stiff, odd, inner):
    rows, cols = stiff_ref.shape
    step = 8

    def some(i):
        for r in range(step):
            x = i * step + r
            stiff[HALO + x, PAD : PAD + cols, :] = spread_stiffness(stiff_ref[pl.ds(x, 1), :])

    loop(rows // step, some)
    for k in range(EARLY):
        operator(k, rows, tiles_of(cols, 2 * k + 2), tiles_of(cols, 2 * k + 3), field, odd, inner, stiff)


def early(field, stiffness):
    rows, cols = stiffness.shape
    big = padded(rows, cols)
    return pl.pallas_call(
        early_kernel,
        in_specs=[VMEM] * 2,
        out_specs=[VMEM] * 4,
        out_shape=[big] * 4,
        input_output_aliases={0: 0},
        compiler_params=params(4),
        cost_estimate=pl.CostEstimate(flops=0, bytes_accessed=0, transcendentals=0),
    )(field, stiffness)


def prepare(slot, x, j, vectors, cols, field, inner, turned, lhs):
    cells = field[HALO + x, PAD : PAD + cols, :].T[:vectors]
    turned[x] = cells
    lhs[slot, 0, :, j * cols : (j + 1) * cols] = cells.astype(BF16)
    lhs[slot, 1, :, j * cols : (j + 1) * cols] = inner[HALO + x, PAD : PAD + cols, :].astype(BF16).T[:vectors]


def multiply(slot, xs, cols, field, inner, lhs, sums):
    for which, ref in enumerate((field, inner)):
        cells = jnp.concatenate([ref[HALO + x, PAD : PAD + cols, :] for x in xs], axis=0)
        high, low = split(cells)
        sums[which] += jnp.dot(
            lhs[slot, which], jnp.concatenate([high, low], axis=1), preferred_element_type=F32
        )


def middle_kernel(vectors, rows, cols, field_in, odd_in, inner_in, stiff_in, one, field, odd, inner, stiff, turned, sums, lhs):
    outside = jnp.where(even(lax.axis_index("row")), HALO + rows, 0)
    for r in range(HALO):
        block = one[r * vectors : (r + 1) * vectors, :]
        field[outside + r, PAD : PAD + cols, :] = lanes_up(block, jnp.zeros((1, cols), F32))
    terms = (field, odd)
    for k in range(DEGREE):
        tiles = tiles_of(cols, 0)
        bends = advances = tiles
        if k < EARLY:
            bends = [y for y in tiles if y not in tiles_of(cols, 2 * k + 2)]
            advances = [y for y in tiles if y not in tiles_of(cols, 2 * k + 3)]
        operator(k, rows, bends, advances, field, odd, inner, stiff)
        clear_cols(terms[(k + 1) % 2], HALO + 2 + 2 * k, HALO + rows - 2 - 2 * k, cols)
    low, high = HALO, rows - HALO
    own = range(PAD, PAD + cols, 8)
    sweep(HALO + low, HALO + high, own, functools.partial(root_bend, terms[DEGREE % 2], stiff, inner))

    first = low + 1
    groups = (high - 1 - first) // GROUP
    sums[...] = jnp.zeros_like(sums)
    final = terms[DEGREE % 2]

    def rows_of(g):
        return [first + g * GROUP + j for j in range(GROUP)]

    def ready(g, slot):
        for j, x in enumerate(rows_of(g)):
            prepare(slot, x, j, vectors, cols, final, inner, turned, lhs)

    ready(0, 0)

    def one(g):
        slot = lax.rem(g, 2)
        multiply(slot, rows_of(g), cols, final, inner, lhs, sums)
        ready(g + 1, 1 - slot)

    loop(groups - 1, one)
    multiply((groups - 1) % 2, rows_of(groups - 1), cols, final, inner, lhs, sums)


def middle(vectors, rows, cols, field, odd, inner, stiff, one):
    big = padded(rows, cols)
    return pl.pallas_call(
        functools.partial(middle_kernel, vectors, rows, cols),
        in_specs=[VMEM] * 5,
        out_specs=[VMEM] * 6,
        out_shape=[
            big,
            big,
            big,
            big,
            jax.ShapeDtypeStruct((rows, vectors, cols), F32),
            jax.ShapeDtypeStruct((2, vectors, 2 * LANES), F32),
        ],
        input_output_aliases={0: 0, 1: 1, 2: 2, 3: 3},
        scratch_shapes=[pltpu.VMEM((2, 2, vectors, GROUP * cols), BF16)],
        compiler_params=params(8),
        cost_estimate=pl.CostEstimate(flops=10**10, bytes_accessed=40 * MIB, transcendentals=0),
    )(field, odd, inner, stiff, one)


def ends_kernel(vectors, rows, cols, field_in, odd_in, inner_in, stiff_in, turned_in, sums_in,
                two, corner_one, whole, field, odd, inner, stiff, turned, packed, sums, lhs):
    row_first = even(lax.axis_index("row"))
    base = 2 * HALO * MARGIN

    def fill(start, row_block, corner):
        for r in range(HALO):
            x = start + r
            weight = corner[base + r : base + r + 1, :]
            if row_block is not None:
                field[x, PAD : PAD + cols, :] = lanes_up(row_block(r), weight)
            stiff[x, PAD : PAD + cols, :] = spread_stiffness(weight)
            for e, y in enumerate((PAD - MARGIN, PAD + cols)):
                piece = corner[(2 * r + e) * MARGIN : (2 * r + e + 1) * MARGIN, :]
                field[x, y : y + MARGIN, :] = piece
                stiff[x, y : y + MARGIN, :] = jnp.broadcast_to(
                    piece[:, vectors : vectors + 1] * (2.0 / HALF), (MARGIN, LANES)
                )

    def second(r):
        ref, at = (two, r) if r < FIRST else (whole, r - FIRST)
        return ref[at * vectors : (at + 1) * vectors, :]

    fill(jnp.where(row_first, HALO + rows, 0), None, corner_one)
    fill(jnp.where(row_first, 0, HALO + rows), second, whole.at[(HALO - FIRST) * vectors :, :])

    def both(low, high, ys, work):
        flip = rows + 2 * HALO

        def side(i):
            x = low + i * (flip - high - low)
            for y in ys:
                work(x, y, 4)
                work(x + 4, y, high - low - 4)

        loop(2, side)

    terms = (field, odd)
    for k in range(DEGREE):
        current, following = terms[k % 2], terms[(k + 1) % 2]
        low = 1 + 2 * k
        tiles = tiles_of(cols, 0)
        both(low, low + HALO, tiles, functools.partial(bend, current, stiff, inner))
        both(low + 1, low + 1 + HALO, tiles, functools.partial(advance, k, current, inner, following))
        clear_cols(following, low + 1, low + 1 + HALO, cols)
        clear_cols(following, rows + 2 * HALO - low - 1 - HALO, rows + 2 * HALO - low - 1, cols)
        clear_rows(following, rows, cols)
    final = terms[DEGREE % 2]
    both(HALO, 2 * HALO, tiles_of(cols, 1), functools.partial(root_bend, final, stiff, inner))

    sums[...] = sums_in[...]
    xs = list(range(HALO + 1)) + list(range(rows - HALO - 1, rows))
    for g in range(0, len(xs), GROUP):
        for j, x in enumerate(xs[g : g + GROUP]):
            prepare(g // GROUP % 2, x, j, vectors, cols, final, inner, turned, lhs)
        multiply(g // GROUP % 2, xs[g : g + GROUP], cols, final, inner, lhs, sums)

    def total(which):
        high, low = sums[which, :, :LANES], sums[which, :, LANES:]
        square = jnp.concatenate([low, jnp.zeros((LANES - vectors, LANES), F32)], axis=0)
        return high + (low + square.T[:vectors])

    gram, image_gram = total(0), total(1)
    i = lax.broadcasted_iota(jnp.int32, (vectors, LANES), 0)
    j = lax.broadcasted_iota(jnp.int32, (vectors, LANES), 1)
    diagonal = jnp.sum(jnp.where(i == j, image_gram, 0.0), axis=1, keepdims=True)
    both_grams = jnp.where(j <= i, gram, image_gram)
    packed[...] = jnp.where(j < vectors, both_grams, jnp.where(j == vectors, diagonal, 0.0))


def ends(vectors, rows, cols, field, odd, inner, stiff, turned, sums, two, corner_one, whole):
    big = padded(rows, cols)
    return pl.pallas_call(
        functools.partial(ends_kernel, vectors, rows, cols),
        in_specs=[VMEM] * 9,
        out_specs=[VMEM] * 6,
        out_shape=[
            big,
            big,
            big,
            big,
            jax.ShapeDtypeStruct((rows, vectors, cols), F32),
            jax.ShapeDtypeStruct((vectors, LANES), F32),
        ],
        input_output_aliases={0: 0, 1: 1, 2: 2, 3: 3, 4: 4},
        scratch_shapes=[
            pltpu.VMEM((2, vectors, 2 * LANES), F32),
            pltpu.VMEM((2, 2, vectors, GROUP * cols), BF16),
        ],
        compiler_params=params(8),
    )(field, odd, inner, stiff, turned, sums, two, corner_one, whole)[4:]


def inverse_factor(gram, vectors):
    lane = lax.broadcasted_iota(jnp.int32, (8, LANES), 1)
    sub = lax.broadcasted_iota(jnp.int32, (8, LANES), 0)
    count = vectors // 8
    blocks = [gram[8 * b : 8 * b + 8] for b in range(count)]

    def spread(values, j):
        return jnp.broadcast_to(values[:, j : j + 1], (8, LANES))

    done = []
    for b in range(count):
        base = 8 * b
        own = (lane >= base) & (lane < base + 8)
        raw = [jnp.broadcast_to(blocks[b][s : s + 1], (8, LANES)) for s in range(8)]
        pivots = [[spread(raw[s], base + k) if k >= s else None for k in range(8)] for s in range(8)]
        below = {t: [spread(blocks[t], base + k) for k in range(8)] for t in range(b + 1, count)}
        rows = [jnp.where(own, jnp.where(lane == base + s, 1.0, 0.0), raw[s]) for s in range(8)]
        for t in range(b + 1, count):
            blocks[t] = jnp.where(own, 0.0, blocks[t])
        finished = jnp.zeros((8, LANES), F32)
        for s in range(8):
            inverse = 1.0 / pivots[s][s]
            for i in range(s + 1, 8):
                m = pivots[s][i] * inverse
                for k in range(i, 8):
                    pivots[i][k] = pivots[i][k] - m * pivots[s][k]
                rows[i] = rows[i] - m * rows[s]
            finished = jnp.where(sub == s, rows[s] * lax.rsqrt(pivots[s][s]), finished)
            for t in range(b + 1, count):
                q = below[t][s] * inverse
                for k in range(s + 1, 8):
                    below[t][k] = below[t][k] - q * pivots[s][k]
                blocks[t] = blocks[t] - q * rows[s]
        done.append(finished)
    full = jnp.concatenate(done, axis=0)
    i = lax.broadcasted_iota(jnp.int32, (vectors, LANES), 0)
    j = lax.broadcasted_iota(jnp.int32, (vectors, LANES), 1)
    return jnp.where(j <= i, full, 0.0)


def finish_kernel(scale, sums_ref, turned, basis_ref, projected_ref, basis, out_sems):
    rows, vectors, cols = turned.shape
    packed = sums_ref[...]
    i = lax.broadcasted_iota(jnp.int32, (vectors, LANES), 0)
    j = lax.broadcasted_iota(jnp.int32, (vectors, LANES), 1)
    square = jnp.concatenate([packed, jnp.zeros((LANES - vectors, LANES), F32)], axis=0)
    flipped = square.T[:vectors]
    gram = jnp.where(j <= i, packed, flipped)
    inverse = inverse_factor(jnp.where(j < vectors, gram, 0.0), vectors)

    high, low = split(inverse[:, :vectors] * scale)
    group = 8
    copies = []
    for x in range(0, rows, group):
        for g in range(0, group, 2):
            pair = jnp.concatenate([turned[x + g], turned[x + g + 1]], axis=1)
            pair_high, pair_low = split(pair)
            result = jnp.dot(high, pair_low, preferred_element_type=F32)
            result += jnp.dot(low, pair_high, preferred_element_type=F32)
            result += jnp.dot(high, pair_high, preferred_element_type=F32)
            basis[:, x + g, :] = result[:, :cols]
            basis[:, x + g + 1, :] = result[:, cols:]
        copies.append(
            pltpu.make_async_copy(
                basis.at[:, pl.ds(x, group), :], basis_ref.at[:, pl.ds(x, group), :], out_sems.at[x // group]
            )
        )
        copies[-1].start()

    image_gram = jnp.where(j > i, packed, jnp.where(j < i, flipped, packed[:, vectors : vectors + 1]))
    image_gram = jnp.where(j < vectors, image_gram, 0.0)
    half = jnp.dot(
        inverse[:, :vectors], image_gram, preferred_element_type=F32, precision=lax.Precision.HIGHEST
    )
    sandwich = lax.dot_general(
        half, inverse, (((1,), (1,)), ((), ())), preferred_element_type=F32, precision=lax.Precision.HIGHEST
    )
    k = lax.broadcasted_iota(jnp.int32, (vectors, vectors), 0)
    m = lax.broadcasted_iota(jnp.int32, (vectors, vectors), 1)
    projected_ref[...] = sandwich * (HALF / (2.0 * TOP)) + jnp.where(k == m, SHIFT / TOP, 0.0)
    for copy in copies:
        copy.wait()


def finish(sums, turned, scale):
    rows, vectors, cols = turned.shape
    return pl.pallas_call(
        functools.partial(finish_kernel, scale),
        in_specs=[VMEM, VMEM],
        out_specs=[HBM, VMEM],
        out_shape=[
            jax.ShapeDtypeStruct((vectors, rows, cols), F32),
            jax.ShapeDtypeStruct((vectors, vectors), F32),
        ],
        scratch_shapes=[
            pltpu.VMEM((vectors, rows, cols), F32),
            pltpu.SemaphoreType.DMA((rows // 8,)),
        ],
        compiler_params=params(8),
    )(sums, turned)


def pairs(count, start):
    found = []
    for i in range(start, count - 1, 2):
        found += [(i, i + 1), (i + 1, i)]
    return found


def all_sum(values, axes):
    count = 1
    for axis in axes:
        count *= lax.axis_size(axis)
    if count & (count - 1):
        return lax.psum(values, axes)
    step = 1
    while step < count:
        values = values + lax.ppermute(values, axes, [(i, i ^ step) for i in range(count)])
        step *= 2
    return values


def body(start_block, stiffness):
    vectors, rows, cols = start_block.shape
    row_count, col_count = lax.axis_size("row"), lax.axis_size("col")
    field, near, far, one, two, rest, stiffness = turn(start_block, stiffness)
    near = lax.ppermute(near, "col", pairs(col_count, 0))
    far = lax.ppermute(far, "col", pairs(col_count, 1))
    one = lax.ppermute(one, "row", pairs(row_count, 0))
    two = lax.ppermute(two, "row", pairs(row_count, 1))
    field, stiff, odd, inner = early(field, stiffness)
    field, stiff, corner_one, whole = corners(vectors, field, stiff, stiffness, near, far, rest)
    corner_one = lax.ppermute(corner_one, "row", pairs(row_count, 0))
    whole = lax.ppermute(whole, "row", pairs(row_count, 1))
    field, odd, inner, stiff, turned, sums = middle(vectors, rows, cols, field, odd, inner, stiff, one)
    turned, sums = ends(vectors, rows, cols, field, odd, inner, stiff, turned, sums, two, corner_one, whole)
    sums = all_sum(sums, ("row", "col"))
    scale = float(rows * row_count * cols * col_count) ** 0.5
    return tuple(finish(sums, turned, scale))


def solution(mesh):
    in_specs = (P(None, "row", "col"), P("row", "col"))
    out_specs = (P(None, "row", "col"), P())
    return jax.shard_map(body, mesh=mesh, in_specs=in_specs, out_specs=out_specs, check_vma=False)
```

```python
import functools
import jax
import jax.numpy as jnp
from jax import lax
from jax.experimental import pallas as pl
from jax.experimental.pallas import tpu as pltpu
from jax.sharding import PartitionSpec as P

DEGREE = 4
TOP = 129.0
CUT = 16.0
SHIFT = 1.0
CENTER = (TOP + CUT) / 2.0
HALF = (TOP - CUT) / 2.0
LEAD = (CENTER - SHIFT) / HALF
HALO = 2 * DEGREE + 1
MARGIN = HALO - 1
FIRST = 5
EARLY = 2
LANES = 128
PAD = 16
GROUP = 4
F32 = jnp.float32
BF16 = jnp.bfloat16
MIB = 2**20
VMEM = pl.BlockSpec(memory_space=pltpu.VMEM)
HBM = pl.BlockSpec(memory_space=pltpu.HBM)


def split(values):
    high = values.astype(BF16)
    low = (values - high.astype(F32)).astype(BF16)
    return high, low


def even(index):
    return lax.rem(index, 2) == 0


def loop(count, work):
    def one(i, carry):
        work(i)
        return carry

    lax.fori_loop(0, count, one, 0)


def params(limit):
    return pltpu.CompilerParams(vmem_limit_bytes=limit * MIB)


def padded(rows, cols):
    return jax.ShapeDtypeStruct((rows + 2 * HALO, cols + 2 * PAD, LANES), F32)


def lanes_up(block, stiff):
    vectors, cols = block.shape
    fill = jnp.zeros((LANES - vectors - 8, cols), F32)
    return jnp.concatenate([block, jnp.broadcast_to(stiff, (8, cols)), fill], axis=0).T


def spread_stiffness(row):
    return jnp.broadcast_to(row * (2.0 / HALF), (LANES, row.shape[1])).T


def turn_kernel(block_ref, stiff_ref, field, near, far, one, two, rest, stiff, held, sems, slab_sems):
    chunks, vectors, step, cols = held.shape
    rows = chunks * step
    col_first, row_first = even(lax.axis_index("col")), even(lax.axis_index("row"))
    stiff_copy = pltpu.make_async_copy(stiff_ref, stiff, sems.at[chunks])
    copies = [
        pltpu.make_async_copy(block_ref.at[:, pl.ds(i * step, step), :], held.at[i], sems.at[i])
        for i in range(chunks)
    ]
    slab_copies = []
    for which, start in enumerate(
        (jnp.where(row_first, rows - HALO, 0), jnp.where(row_first, 0, rows - HALO))
    ):
        for r in range(HALO):
            out, at = (one, r) if which == 0 else (two, r) if r < FIRST else (rest, r - FIRST)
            slab_copies.append(
                pltpu.make_async_copy(
                    block_ref.at[:, start + r, :], out.at[pl.ds(at * vectors, vectors), :], slab_sems.at[which, r]
                )
            )
    for copy in [stiff_copy] + copies + slab_copies:
        copy.start()
    stiff_copy.wait()
    for i in range(chunks):
        copies[i].wait()
        for r in range(step):
            x = i * step + r
            turned = lanes_up(held[i, :, r, :], stiff[x : x + 1, :])
            field[HALO + x, PAD : PAD + cols, :] = turned
            head, tail = turned[:HALO], turned[cols - HALO :]
            near[x * HALO : (x + 1) * HALO, :] = jnp.where(col_first, tail, head)
            far[x * HALO : (x + 1) * HALO, :] = jnp.where(col_first, head, tail)
    for copy in slab_copies:
        copy.wait()


def turn(block, stiffness):
    vectors, rows, cols = block.shape
    side = jax.ShapeDtypeStruct((rows * HALO, LANES), F32)

    def slab(count):
        return jax.ShapeDtypeStruct((count * vectors, cols), F32)

    step = 16
    return pl.pallas_call(
        turn_kernel,
        in_specs=[HBM] * 2,
        out_specs=[VMEM] * 7,
        out_shape=[
            padded(rows, cols),
            side,
            side,
            slab(HALO),
            slab(FIRST),
            slab(HALO - FIRST),
            jax.ShapeDtypeStruct(stiffness.shape, F32),
        ],
        scratch_shapes=[
            pltpu.VMEM((rows // step, vectors, step, cols), F32),
            pltpu.SemaphoreType.DMA((rows // step + 1,)),
            pltpu.SemaphoreType.DMA((2, HALO)),
        ],
        compiler_params=params(8),
        cost_estimate=pl.CostEstimate(flops=0, bytes_accessed=4 * vectors * rows * cols * 2, transcendentals=0),
    )(
        pltpu.with_memory_space_constraint(block, pltpu.HBM),
        pltpu.with_memory_space_constraint(stiffness, pltpu.HBM),
    )


def corner_kernel(vectors, field_in, stiff_in, stiff_ref, near, far, rest, field, stiff, one, whole):
    rows, cols = stiff_ref.shape
    col_first, row_first = even(lax.axis_index("col")), even(lax.axis_index("row"))
    left = jnp.where(lax.axis_index("col") == 0, 0.0, 1.0)
    right = jnp.where(lax.axis_index("col") == lax.axis_size("col") - 1, 0.0, 1.0)
    step = 8
    ends = (PAD - MARGIN, PAD + cols)

    def some(i):
        for r in range(step):
            x = i * step + r
            a, b = near[pl.ds(x * HALO, HALO), :], far[pl.ds(x * HALO, HALO), :]
            field[HALO + x, PAD - HALO : PAD, :] = jnp.where(col_first, b, a) * left
            field[HALO + x, PAD + cols : PAD + cols + HALO, :] = jnp.where(col_first, a, b) * right
        for r in range(step):
            x = HALO + i * step + r
            for y in ends:
                lane = field[x, y : y + MARGIN, vectors : vectors + 1] * (2.0 / HALF)
                stiff[x, y : y + MARGIN, :] = jnp.broadcast_to(lane, (MARGIN, LANES))

    loop(rows // step, some)
    last = rows - HALO
    size = rest.shape[0]
    whole[:size, :] = rest[...]
    two = whole.at[size:, :]
    for out, start in ((one, jnp.where(row_first, last, 0)), (two, jnp.where(row_first, 0, last))):
        for r in range(HALO):
            for e, y in enumerate(ends):
                out[(2 * r + e) * MARGIN : (2 * r + e + 1) * MARGIN, :] = field[HALO + start + r, y : y + MARGIN, :]
        base = 2 * HALO * MARGIN
        out[base:, :] = jnp.zeros((out.shape[0] - base, LANES), F32)
    base = 2 * HALO * MARGIN
    head, tail = stiff_ref[:HALO, :], stiff_ref[last:, :]
    one[base : base + HALO, :] = jnp.where(row_first, tail, head)
    two[base : base + HALO, :] = jnp.where(row_first, head, tail)


def corners(vectors, field, stiff, stiffness, near, far, rest):
    rows, cols = stiffness.shape
    corner = jax.ShapeDtypeStruct((2 * HALO * MARGIN + 16, LANES), F32)
    whole = jax.ShapeDtypeStruct((rest.shape[0] + corner.shape[0], LANES), F32)
    return pl.pallas_call(
        functools.partial(corner_kernel, vectors),
        in_specs=[VMEM] * 6,
        out_specs=[VMEM] * 4,
        out_shape=[padded(rows, cols), padded(rows, cols), corner, whole],
        input_output_aliases={0: 0, 1: 1},
        compiler_params=params(4),
        cost_estimate=pl.CostEstimate(flops=0, bytes_accessed=0, transcendentals=0),
    )(field, stiff, stiffness, near, far, rest)


def around(ref, x, y, step):
    mid = ref[pl.ds(x - 1, step + 2), pl.ds(y, 8), :]
    left = ref[pl.ds(x, step), pl.ds(y - 1, 8), :]
    right = ref[pl.ds(x, step), pl.ds(y + 1, 8), :]
    return ((mid[:-2] + mid[2:]) + (left + right)) - 4.0 * mid[1:-1]


def bend(field, stiff, inner, x, y, step):
    at = (pl.ds(x, step), pl.ds(y, 8))
    inner[*at, :] = stiff[*at, :] * around(field, x, y, step)


def advance(k, current, inner, following, x, y, step):
    at = (pl.ds(x, step), pl.ds(y, 8))
    image = around(inner, x, y, step)
    here = current[*at, :]
    if k == 0:
        following[*at, :] = LEAD * here - 0.5 * image
    else:
        following[*at, :] = (2.0 * LEAD * here - following[*at, :]) - image


def root_bend(field, stiff, inner, x, y, step):
    at = (pl.ds(x, step), pl.ds(y, 8))
    weight = stiff[*at, :]
    inner[*at, :] = weight * lax.rsqrt(weight) * around(field, x, y, step)


def sweep(low, high, ys, work):
    step, unroll = 4, 4

    def trip(i):
        for u in range(unroll):
            for y in ys:
                work(low + (i * unroll + u) * step, y, step)

    trips = (high - low) // (step * unroll)
    loop(trips, trip)
    for x in range(low + trips * unroll * step, high, step):
        for y in ys:
            work(x, y, min(step, high - x))


def clear_cols(field, low, height, cols):
    col, count = lax.axis_index("col"), lax.axis_size("col")

    def at(start):
        field[pl.ds(low, height), start : start + MARGIN, :] = jnp.zeros((height, MARGIN, LANES), F32)

    pl.when(col == 0)(lambda: at(PAD - MARGIN))
    pl.when(col == count - 1)(lambda: at(PAD + cols))


def clear_rows(field, rows, cols):
    row, count = lax.axis_index("row"), lax.axis_size("row")

    def at(start):
        wide = cols + 2 * MARGIN
        for x in range(start, start + HALO):
            field[x, PAD - MARGIN : PAD + cols + MARGIN, :] = jnp.zeros((wide, LANES), F32)

    pl.when(row == 0)(lambda: at(0))
    pl.when(row == count - 1)(lambda: at(HALO + rows))


def tiles_of(cols, inset):
    return range(PAD - MARGIN + 8 * inset, PAD + cols + MARGIN - 8 * inset, 8)


def operator(k, rows, bends, advances, field, odd, inner, stiff):
    current, following = ((field, odd), (odd, field))[k % 2]
    low, high = HALO + 1 + 2 * k, HALO + rows - 1 - 2 * k
    sweep(low, high, bends, functools.partial(bend, current, stiff, inner))
    sweep(low + 1, high - 1, advances, functools.partial(advance, k, current, inner, following))


def early_kernel(field_in, stiff_ref, field, stiff, odd, inner):
    rows, cols = stiff_ref.shape
    step = 8

    def some(i):
        for r in range(step):
            x = i * step + r
            stiff[HALO + x, PAD : PAD + cols, :] = spread_stiffness(stiff_ref[pl.ds(x, 1), :])

    loop(rows // step, some)
    for k in range(EARLY):
        operator(k, rows, tiles_of(cols, 2 * k + 2), tiles_of(cols, 2 * k + 3), field, odd, inner, stiff)


def early(field, stiffness):
    rows, cols = stiffness.shape
    big = padded(rows, cols)
    return pl.pallas_call(
        early_kernel,
        in_specs=[VMEM] * 2,
        out_specs=[VMEM] * 4,
        out_shape=[big] * 4,
        input_output_aliases={0: 0},
        compiler_params=params(4),
        cost_estimate=pl.CostEstimate(flops=0, bytes_accessed=0, transcendentals=0),
    )(field, stiffness)


def prepare(slot, x, j, vectors, cols, field, inner, turned, lhs):
    cells = field[HALO + x, PAD : PAD + cols, :].T[:vectors]
    turned[x] = cells
    lhs[slot, 0, :, j * cols : (j + 1) * cols] = cells.astype(BF16)
    lhs[slot, 1, :, j * cols : (j + 1) * cols] = inner[HALO + x, PAD : PAD + cols, :].astype(BF16).T[:vectors]


def multiply(slot, xs, cols, field, inner, lhs, sums):
    width = len(xs) * cols
    for which, ref in enumerate((field, inner)):
        cells = jnp.concatenate([ref[HALO + x, PAD : PAD + cols, :] for x in xs], axis=0)
        high, low = split(cells)
        sums[which] += jnp.dot(
            lhs[slot, which, :, :width], jnp.concatenate([high, low], axis=1), preferred_element_type=F32
        )


def middle_kernel(vectors, rows, cols, field_in, odd_in, inner_in, stiff_in, one, field, odd, inner, stiff, turned, sums, lhs):
    outside = jnp.where(even(lax.axis_index("row")), HALO + rows, 0)
    for r in range(HALO):
        block = one[r * vectors : (r + 1) * vectors, :]
        field[outside + r, PAD : PAD + cols, :] = lanes_up(block, jnp.zeros((1, cols), F32))
    terms = (field, odd)
    for k in range(DEGREE):
        tiles = tiles_of(cols, 0)
        bends = advances = tiles
        if k < EARLY:
            bends = [y for y in tiles if y not in tiles_of(cols, 2 * k + 2)]
            advances = [y for y in tiles if y not in tiles_of(cols, 2 * k + 3)]
        operator(k, rows, bends, advances, field, odd, inner, stiff)
        clear_cols(terms[(k + 1) % 2], HALO + 2 + 2 * k, rows - 4 - 4 * k, cols)
    low, high = HALO, rows - HALO
    own = range(PAD, PAD + cols, 8)
    sweep(HALO + low, HALO + high, own, functools.partial(root_bend, terms[DEGREE % 2], stiff, inner))

    first = low + 1
    groups = (high - 1 - first) // GROUP
    sums[...] = jnp.zeros_like(sums)
    final = terms[DEGREE % 2]

    def rows_of(g):
        return [first + g * GROUP + j for j in range(GROUP)]

    def ready(g, slot):
        for j, x in enumerate(rows_of(g)):
            prepare(slot, x, j, vectors, cols, final, inner, turned, lhs)

    ready(0, 0)

    def one(g):
        slot = lax.rem(g, 2)
        multiply(slot, rows_of(g), cols, final, inner, lhs, sums)
        ready(g + 1, 1 - slot)

    loop(groups - 1, one)
    multiply((groups - 1) % 2, rows_of(groups - 1), cols, final, inner, lhs, sums)


def middle(vectors, rows, cols, field, odd, inner, stiff, one):
    big = padded(rows, cols)
    return pl.pallas_call(
        functools.partial(middle_kernel, vectors, rows, cols),
        in_specs=[VMEM] * 5,
        out_specs=[VMEM] * 6,
        out_shape=[
            big,
            big,
            big,
            big,
            jax.ShapeDtypeStruct((rows, vectors, cols), F32),
            jax.ShapeDtypeStruct((2, vectors, 2 * LANES), F32),
        ],
        input_output_aliases={0: 0, 1: 1, 2: 2, 3: 3},
        scratch_shapes=[pltpu.VMEM((2, 2, vectors, GROUP * cols), BF16)],
        compiler_params=params(8),
        cost_estimate=pl.CostEstimate(flops=10**10, bytes_accessed=40 * MIB, transcendentals=0),
    )(field, odd, inner, stiff, one)


def end_kernel(vectors, rows, cols, last, field_in, odd_in, inner_in, stiff_in, turned_in, sums_in,
               *refs):
    if last:
        two, corner, field, odd, inner, stiff, turned, packed, sums, lhs = refs
        corner_at = (HALO - FIRST) * vectors
    else:
        corner, field, odd, inner, stiff, turned, sums, lhs = refs
        corner_at = 0
    row_first = even(lax.axis_index("row"))
    side = jnp.where(row_first, 0 if last else 1, 1 if last else 0)
    base = corner_at + 2 * HALO * MARGIN
    start = side * (HALO + rows)
    for r in range(HALO):
        x = start + r
        weight = corner[base + r : base + r + 1, :]
        if last:
            ref, at = (two, r) if r < FIRST else (corner, r - FIRST)
            block = ref[at * vectors : (at + 1) * vectors, :]
            field[x, PAD : PAD + cols, :] = lanes_up(block, weight)
        stiff[x, PAD : PAD + cols, :] = spread_stiffness(weight)
        for e, y in enumerate((PAD - MARGIN, PAD + cols)):
            at = corner_at + (2 * r + e) * MARGIN
            piece = corner[at : at + MARGIN, :]
            field[x, y : y + MARGIN, :] = piece
            stiff[x, y : y + MARGIN, :] = jnp.broadcast_to(
                piece[:, vectors : vectors + 1] * (2.0 / HALF), (MARGIN, LANES)
            )
    if last:
        clear_rows(field, rows, cols)
        clear_rows(stiff, rows, cols)

    def some_rows(low, ys, work):
        x = low + side * (rows + HALO - 2 * low)
        for y in ys:
            work(x, y, 4)
            work(x + 4, y, HALO - 4)

    terms = (field, odd)
    for k in range(DEGREE):
        current, following = terms[k % 2], terms[(k + 1) % 2]
        low = 1 + 2 * k
        tiles = tiles_of(cols, 0)
        some_rows(low, tiles, functools.partial(bend, current, stiff, inner))
        some_rows(low + 1, tiles, functools.partial(advance, k, current, inner, following))
        clear_cols(following, low + 1 + side * (rows + HALO - 2 * low - 2), HALO, cols)
        if last:
            clear_rows(following, rows, cols)
    final = terms[DEGREE % 2]
    some_rows(HALO, tiles_of(cols, 1), functools.partial(root_bend, final, stiff, inner))

    if last:
        sums[...] = sums_in[...]
    first = side * (rows - HALO - 1)
    for g in range(0, HALO + 1, GROUP):
        xs = [first + x for x in range(g, min(g + GROUP, HALO + 1))]
        for j, x in enumerate(xs):
            prepare(g // GROUP % 2, x, j, vectors, cols, final, inner, turned, lhs)
        multiply(g // GROUP % 2, xs, cols, final, inner, lhs, sums)
    if not last:
        return

    def total(which):
        high, low = sums[which, :, :LANES], sums[which, :, LANES:]
        square = jnp.concatenate([low, jnp.zeros((LANES - vectors, LANES), F32)], axis=0)
        return high + (low + square.T[:vectors])

    gram, image_gram = total(0), total(1)
    i = lax.broadcasted_iota(jnp.int32, (vectors, LANES), 0)
    j = lax.broadcasted_iota(jnp.int32, (vectors, LANES), 1)
    diagonal = jnp.sum(jnp.where(i == j, image_gram, 0.0), axis=1, keepdims=True)
    both_grams = jnp.where(j <= i, gram, image_gram)
    packed[...] = jnp.where(j < vectors, both_grams, jnp.where(j == vectors, diagonal, 0.0))


def end(vectors, rows, cols, state, halo):
    last = len(halo) > 1
    big = padded(rows, cols)
    shapes = [big] * 4 + [jax.ShapeDtypeStruct((rows, vectors, cols), F32)]
    sums = (2, vectors, 2 * LANES)
    shapes.append(jax.ShapeDtypeStruct((vectors, LANES) if last else sums, F32))
    return pl.pallas_call(
        functools.partial(end_kernel, vectors, rows, cols, last),
        in_specs=[VMEM] * (6 + len(halo)),
        out_specs=[VMEM] * 6,
        out_shape=shapes,
        input_output_aliases={i: i for i in range(5 if last else 6)},
        scratch_shapes=([pltpu.VMEM(sums, F32)] if last else [])
        + [pltpu.VMEM((2, 2, vectors, GROUP * cols), BF16)],
        compiler_params=params(8),
    )(*state, *halo)


def inverse_factor(gram, vectors):
    lane = lax.broadcasted_iota(jnp.int32, (8, LANES), 1)
    sub = lax.broadcasted_iota(jnp.int32, (8, LANES), 0)
    count = vectors // 8
    blocks = [gram[8 * b : 8 * b + 8] for b in range(count)]

    def spread(values, j):
        return jnp.broadcast_to(values[:, j : j + 1], (8, LANES))

    done = []
    for b in range(count):
        base = 8 * b
        own = (lane >= base) & (lane < base + 8)
        raw = [jnp.broadcast_to(blocks[b][s : s + 1], (8, LANES)) for s in range(8)]
        pivots = [[spread(raw[s], base + k) if k >= s else None for k in range(8)] for s in range(8)]
        below = {t: [spread(blocks[t], base + k) for k in range(8)] for t in range(b + 1, count)}
        rows = [jnp.where(own, jnp.where(lane == base + s, 1.0, 0.0), raw[s]) for s in range(8)]
        for t in range(b + 1, count):
            blocks[t] = jnp.where(own, 0.0, blocks[t])
        finished = jnp.zeros((8, LANES), F32)
        for s in range(8):
            inverse = 1.0 / pivots[s][s]
            for i in range(s + 1, 8):
                m = pivots[s][i] * inverse
                for k in range(i, 8):
                    pivots[i][k] = pivots[i][k] - m * pivots[s][k]
                rows[i] = rows[i] - m * rows[s]
            finished = jnp.where(sub == s, rows[s] * lax.rsqrt(pivots[s][s]), finished)
            for t in range(b + 1, count):
                q = below[t][s] * inverse
                for k in range(s + 1, 8):
                    below[t][k] = below[t][k] - q * pivots[s][k]
                blocks[t] = blocks[t] - q * rows[s]
        done.append(finished)
    full = jnp.concatenate(done, axis=0)
    i = lax.broadcasted_iota(jnp.int32, (vectors, LANES), 0)
    j = lax.broadcasted_iota(jnp.int32, (vectors, LANES), 1)
    return jnp.where(j <= i, full, 0.0)


def finish_kernel(scale, sums_ref, turned, basis_ref, projected_ref, basis, out_sems):
    rows, vectors, cols = turned.shape
    packed = sums_ref[...]
    i = lax.broadcasted_iota(jnp.int32, (vectors, LANES), 0)
    j = lax.broadcasted_iota(jnp.int32, (vectors, LANES), 1)
    square = jnp.concatenate([packed, jnp.zeros((LANES - vectors, LANES), F32)], axis=0)
    flipped = square.T[:vectors]
    gram = jnp.where(j <= i, packed, flipped)
    inverse = inverse_factor(jnp.where(j < vectors, gram, 0.0), vectors)

    high, low = split(inverse[:, :vectors] * scale)
    group = 8
    copies = []
    for x in range(0, rows, group):
        for g in range(0, group, 2):
            pair = jnp.concatenate([turned[x + g], turned[x + g + 1]], axis=1)
            pair_high, pair_low = split(pair)
            result = jnp.dot(high, pair_low, preferred_element_type=F32)
            result += jnp.dot(low, pair_high, preferred_element_type=F32)
            result += jnp.dot(high, pair_high, preferred_element_type=F32)
            basis[:, x + g, :] = result[:, :cols]
            basis[:, x + g + 1, :] = result[:, cols:]
        copies.append(
            pltpu.make_async_copy(
                basis.at[:, pl.ds(x, group), :], basis_ref.at[:, pl.ds(x, group), :], out_sems.at[x // group]
            )
        )
        copies[-1].start()

    image_gram = jnp.where(j > i, packed, jnp.where(j < i, flipped, packed[:, vectors : vectors + 1]))
    image_gram = jnp.where(j < vectors, image_gram, 0.0)
    half = jnp.dot(
        inverse[:, :vectors], image_gram, preferred_element_type=F32, precision=lax.Precision.HIGHEST
    )
    sandwich = lax.dot_general(
        half, inverse, (((1,), (1,)), ((), ())), preferred_element_type=F32, precision=lax.Precision.HIGHEST
    )
    k = lax.broadcasted_iota(jnp.int32, (vectors, vectors), 0)
    m = lax.broadcasted_iota(jnp.int32, (vectors, vectors), 1)
    projected_ref[...] = sandwich * (HALF / (2.0 * TOP)) + jnp.where(k == m, SHIFT / TOP, 0.0)
    for copy in copies:
        copy.wait()


def finish(sums, turned, scale):
    rows, vectors, cols = turned.shape
    return pl.pallas_call(
        functools.partial(finish_kernel, scale),
        in_specs=[VMEM, VMEM],
        out_specs=[HBM, VMEM],
        out_shape=[
            jax.ShapeDtypeStruct((vectors, rows, cols), F32),
            jax.ShapeDtypeStruct((vectors, vectors), F32),
        ],
        scratch_shapes=[
            pltpu.VMEM((vectors, rows, cols), F32),
            pltpu.SemaphoreType.DMA((rows // 8,)),
        ],
        compiler_params=params(8),
    )(sums, turned)


def pairs(count, start):
    found = []
    for i in range(start, start + count - 1, 2):
        found += [(i % count, (i + 1) % count), ((i + 1) % count, i % count)]
    return found


def inner_pairs(row_count, col_count):
    found = []
    for r in range(row_count):
        for c in range(col_count):
            beside = c + 1 if c % 2 else c - 1
            there = (r, beside) if 0 <= beside < col_count else (r ^ (row_count // 2), c)
            found.append((r * col_count + c, there[0] * col_count + there[1]))
    return found


def all_sum(values, axes):
    count = 1
    for axis in axes:
        count *= lax.axis_size(axis)
    if count & (count - 1):
        return lax.psum(values, axes)
    step = 1
    while step < count:
        values = values + lax.ppermute(values, axes, [(i, i ^ (step | 1)) for i in range(count)])
        step *= 2
    return values


def body(start_block, stiffness):
    vectors, rows, cols = start_block.shape
    row_count, col_count = lax.axis_size("row"), lax.axis_size("col")
    field, near, far, one, two, rest, stiffness = turn(start_block, stiffness)
    near = lax.ppermute(near, "col", pairs(col_count, 0))
    far = lax.ppermute(far, ("row", "col"), inner_pairs(row_count, col_count))
    one = lax.ppermute(one, "row", pairs(row_count, 0))
    two = lax.ppermute(two, "row", pairs(row_count, 1))
    field, stiff, odd, inner = early(field, stiffness)
    field, stiff, corner_one, whole = corners(vectors, field, stiff, stiffness, near, far, rest)
    corner_one = lax.ppermute(corner_one, "row", pairs(row_count, 0))
    whole = lax.ppermute(whole, "row", pairs(row_count, 1))
    state = middle(vectors, rows, cols, field, odd, inner, stiff, one)
    state = end(vectors, rows, cols, state, (corner_one,))
    *_, turned, sums = end(vectors, rows, cols, state, (two, whole))
    sums = all_sum(sums, ("row", "col"))
    scale = float(rows * row_count * cols * col_count) ** 0.5
    return tuple(finish(sums, turned, scale))


def solution(mesh):
    in_specs = (P(None, "row", "col"), P("row", "col"))
    out_specs = (P(None, "row", "col"), P())
    return jax.shard_map(body, mesh=mesh, in_specs=in_specs, out_specs=out_specs, check_vma=False)
```

```python
import functools
import jax
import jax.numpy as jnp
from jax import lax
from jax.experimental import pallas as pl
from jax.experimental.pallas import tpu as pltpu
from jax.sharding import PartitionSpec as P

DEGREE = 4
TOP = 129.0
CUT = 16.0
SHIFT = 1.0
CENTER = (TOP + CUT) / 2.0
HALF = (TOP - CUT) / 2.0
LEAD = (CENTER - SHIFT) / HALF
HALO = 2 * DEGREE + 1
MARGIN = HALO - 1
FIRST = 5
EARLY = 2
LANES = 128
PAD = 16
GROUP = 4
F32 = jnp.float32
BF16 = jnp.bfloat16
MIB = 2**20
VMEM = pl.BlockSpec(memory_space=pltpu.VMEM)
HBM = pl.BlockSpec(memory_space=pltpu.HBM)


def split(values):
    high = values.astype(BF16)
    low = (values - high.astype(F32)).astype(BF16)
    return high, low


def even(index):
    return lax.rem(index, 2) == 0


def loop(count, work):
    def one(i, carry):
        work(i)
        return carry

    lax.fori_loop(0, count, one, 0)


def params(limit):
    return pltpu.CompilerParams(vmem_limit_bytes=limit * MIB)


def padded(rows, cols):
    return jax.ShapeDtypeStruct((rows + 2 * HALO, cols + 2 * PAD, LANES), F32)


def lanes_up(block, stiff):
    vectors, cols = block.shape
    fill = jnp.zeros((LANES - vectors - 8, cols), F32)
    return jnp.concatenate([block, jnp.broadcast_to(stiff, (8, cols)), fill], axis=0).T


def spread_stiffness(row):
    return jnp.broadcast_to(row * (2.0 / HALF), (LANES, row.shape[1])).T


def turn_kernel(block_ref, stiff_ref, field, near, far, one, two, rest, stiff, held, sems, slab_sems):
    chunks, vectors, step, cols = held.shape
    rows = chunks * step
    col_first, row_first = even(lax.axis_index("col")), even(lax.axis_index("row"))
    stiff_copy = pltpu.make_async_copy(stiff_ref, stiff, sems.at[chunks])
    copies = [
        pltpu.make_async_copy(block_ref.at[:, pl.ds(i * step, step), :], held.at[i], sems.at[i])
        for i in range(chunks)
    ]
    slab_copies = []
    for which, start in enumerate(
        (jnp.where(row_first, rows - HALO, 0), jnp.where(row_first, 0, rows - HALO))
    ):
        for r in range(HALO):
            out, at = (one, r) if which == 0 else (two, r) if r < FIRST else (rest, r - FIRST)
            slab_copies.append(
                pltpu.make_async_copy(
                    block_ref.at[:, start + r, :], out.at[pl.ds(at * vectors, vectors), :], slab_sems.at[which, r]
                )
            )
    for copy in [stiff_copy] + copies + slab_copies:
        copy.start()
    stiff_copy.wait()
    for i in range(chunks):
        copies[i].wait()
        for r in range(step):
            x = i * step + r
            if r % 8 == 0:
                eight = jnp.swapaxes(held[i, :, r : r + 8, :], 0, 1)
            turned = lanes_up(eight[r % 8], stiff[x : x + 1, :])
            field[HALO + x, PAD : PAD + cols, :] = turned
            head, tail = turned[:HALO], turned[cols - HALO :]
            near[x * HALO : (x + 1) * HALO, :] = jnp.where(col_first, tail, head)
            far[x * HALO : (x + 1) * HALO, :] = jnp.where(col_first, head, tail)
    for copy in slab_copies:
        copy.wait()


def turn(block, stiffness):
    vectors, rows, cols = block.shape
    side = jax.ShapeDtypeStruct((rows * HALO, LANES), F32)

    def slab(count):
        return jax.ShapeDtypeStruct((count * vectors, cols), F32)

    step = 16
    return pl.pallas_call(
        turn_kernel,
        in_specs=[HBM] * 2,
        out_specs=[VMEM] * 7,
        out_shape=[
            padded(rows, cols),
            side,
            side,
            slab(HALO),
            slab(FIRST),
            slab(HALO - FIRST),
            jax.ShapeDtypeStruct(stiffness.shape, F32),
        ],
        scratch_shapes=[
            pltpu.VMEM((rows // step, vectors, step, cols), F32),
            pltpu.SemaphoreType.DMA((rows // step + 1,)),
            pltpu.SemaphoreType.DMA((2, HALO)),
        ],
        compiler_params=params(8),
        cost_estimate=pl.CostEstimate(flops=0, bytes_accessed=4 * vectors * rows * cols * 2, transcendentals=0),
    )(
        pltpu.with_memory_space_constraint(block, pltpu.HBM),
        pltpu.with_memory_space_constraint(stiffness, pltpu.HBM),
    )


def corner_kernel(vectors, field_in, stiff_in, stiff_ref, near, far, rest, field, stiff, one, whole):
    rows, cols = stiff_ref.shape
    col_first, row_first = even(lax.axis_index("col")), even(lax.axis_index("row"))
    left = jnp.where(lax.axis_index("col") == 0, 0.0, 1.0)
    right = jnp.where(lax.axis_index("col") == lax.axis_size("col") - 1, 0.0, 1.0)
    step = 8
    ends = (PAD - MARGIN, PAD + cols)

    def some(i):
        for r in range(step):
            x = i * step + r
            a, b = near[pl.ds(x * HALO, HALO), :], far[pl.ds(x * HALO, HALO), :]
            field[HALO + x, PAD - HALO : PAD, :] = jnp.where(col_first, b, a) * left
            field[HALO + x, PAD + cols : PAD + cols + HALO, :] = jnp.where(col_first, a, b) * right
        for r in range(step):
            x = HALO + i * step + r
            for y in ends:
                lane = field[x, y : y + MARGIN, vectors : vectors + 1] * (2.0 / HALF)
                stiff[x, y : y + MARGIN, :] = jnp.broadcast_to(lane, (MARGIN, LANES))

    loop(rows // step, some)
    last = rows - HALO
    size = rest.shape[0]
    whole[:size, :] = rest[...]
    two = whole.at[size:, :]
    for out, start in ((one, jnp.where(row_first, last, 0)), (two, jnp.where(row_first, 0, last))):
        for r in range(HALO):
            for e, y in enumerate(ends):
                out[(2 * r + e) * MARGIN : (2 * r + e + 1) * MARGIN, :] = field[HALO + start + r, y : y + MARGIN, :]
        base = 2 * HALO * MARGIN
        out[base:, :] = jnp.zeros((out.shape[0] - base, LANES), F32)
    base = 2 * HALO * MARGIN
    head, tail = stiff_ref[:HALO, :], stiff_ref[last:, :]
    one[base : base + HALO, :] = jnp.where(row_first, tail, head)
    two[base : base + HALO, :] = jnp.where(row_first, head, tail)


def corners(vectors, field, stiff, stiffness, near, far, rest):
    rows, cols = stiffness.shape
    corner = jax.ShapeDtypeStruct((2 * HALO * MARGIN + 16, LANES), F32)
    whole = jax.ShapeDtypeStruct((rest.shape[0] + corner.shape[0], LANES), F32)
    return pl.pallas_call(
        functools.partial(corner_kernel, vectors),
        in_specs=[VMEM] * 6,
        out_specs=[VMEM] * 4,
        out_shape=[padded(rows, cols), padded(rows, cols), corner, whole],
        input_output_aliases={0: 0, 1: 1},
        compiler_params=params(4),
        cost_estimate=pl.CostEstimate(flops=0, bytes_accessed=0, transcendentals=0),
    )(field, stiff, stiffness, near, far, rest)


def around(ref, x, y, step):
    mid = ref[pl.ds(x - 1, step + 2), pl.ds(y, 8), :]
    left = ref[pl.ds(x, step), pl.ds(y - 1, 8), :]
    right = ref[pl.ds(x, step), pl.ds(y + 1, 8), :]
    return ((mid[:-2] + mid[2:]) + (left + right)) - 4.0 * mid[1:-1]


def bend(field, stiff, inner, x, y, step):
    at = (pl.ds(x, step), pl.ds(y, 8))
    inner[*at, :] = stiff[*at, :] * around(field, x, y, step)


def advance(k, current, inner, following, x, y, step):
    at = (pl.ds(x, step), pl.ds(y, 8))
    image = around(inner, x, y, step)
    here = current[*at, :]
    if k == 0:
        following[*at, :] = LEAD * here - 0.5 * image
    else:
        following[*at, :] = (2.0 * LEAD * here - following[*at, :]) - image


def root_bend(field, stiff, inner, x, y, step):
    at = (pl.ds(x, step), pl.ds(y, 8))
    weight = stiff[*at, :]
    inner[*at, :] = weight * lax.rsqrt(weight) * around(field, x, y, step)


def sweep(low, high, ys, work):
    step, unroll = 4, 4

    def trip(i):
        for u in range(unroll):
            for y in ys:
                work(low + (i * unroll + u) * step, y, step)

    trips = (high - low) // (step * unroll)
    loop(trips, trip)
    for x in range(low + trips * unroll * step, high, step):
        for y in ys:
            work(x, y, min(step, high - x))


def clear_cols(field, low, height, cols):
    col, count = lax.axis_index("col"), lax.axis_size("col")

    def at(start):
        field[pl.ds(low, height), start : start + MARGIN, :] = jnp.zeros((height, MARGIN, LANES), F32)

    pl.when(col == 0)(lambda: at(PAD - MARGIN))
    pl.when(col == count - 1)(lambda: at(PAD + cols))


def clear_rows(field, rows, cols):
    row, count = lax.axis_index("row"), lax.axis_size("row")

    def at(start):
        wide = cols + 2 * MARGIN
        for x in range(start, start + HALO):
            field[x, PAD - MARGIN : PAD + cols + MARGIN, :] = jnp.zeros((wide, LANES), F32)

    pl.when(row == 0)(lambda: at(0))
    pl.when(row == count - 1)(lambda: at(HALO + rows))


def tiles_of(cols, inset):
    return range(PAD - MARGIN + 8 * inset, PAD + cols + MARGIN - 8 * inset, 8)


def operator(k, rows, bends, advances, field, odd, inner, stiff):
    current, following = ((field, odd), (odd, field))[k % 2]
    low, high = HALO + 1 + 2 * k, HALO + rows - 1 - 2 * k
    sweep(low, high, bends, functools.partial(bend, current, stiff, inner))
    sweep(low + 1, high - 1, advances, functools.partial(advance, k, current, inner, following))


def early_kernel(field_in, stiff_ref, field, stiff, odd, inner):
    rows, cols = stiff_ref.shape
    step = 32

    def some(i):
        for r in range(step):
            x = i * step + r
            stiff[HALO + x, PAD : PAD + cols, :] = spread_stiffness(stiff_ref[pl.ds(x, 1), :])

    loop(rows // step, some)
    for k in range(EARLY):
        operator(k, rows, tiles_of(cols, 2 * k + 2), tiles_of(cols, 2 * k + 3), field, odd, inner, stiff)


def early(field, stiffness):
    rows, cols = stiffness.shape
    big = padded(rows, cols)
    return pl.pallas_call(
        early_kernel,
        in_specs=[VMEM] * 2,
        out_specs=[VMEM] * 4,
        out_shape=[big] * 4,
        input_output_aliases={0: 0},
        compiler_params=params(4),
        cost_estimate=pl.CostEstimate(flops=0, bytes_accessed=0, transcendentals=0),
    )(field, stiffness)


def prepare(slot, x, j, vectors, cols, field, inner, turned, lhs):
    cells = field[HALO + x, PAD : PAD + cols, :].T[:vectors]
    turned[x] = cells
    lhs[slot, 0, :, j * cols : (j + 1) * cols] = cells.astype(BF16)
    lhs[slot, 1, :, j * cols : (j + 1) * cols] = inner[HALO + x, PAD : PAD + cols, :].astype(BF16).T[:vectors]


def multiply(slot, xs, cols, field, inner, lhs, sums):
    width = len(xs) * cols
    for which, ref in enumerate((field, inner)):
        cells = jnp.concatenate([ref[HALO + x, PAD : PAD + cols, :] for x in xs], axis=0)
        high, low = split(cells)
        sums[which] += jnp.dot(
            lhs[slot, which, :, :width], jnp.concatenate([high, low], axis=1), preferred_element_type=F32
        )


def middle_kernel(vectors, rows, cols, field_in, odd_in, inner_in, stiff_in, one, field, odd, inner, stiff, turned, sums, lhs):
    outside = jnp.where(even(lax.axis_index("row")), HALO + rows, 0)
    for r in range(HALO):
        block = one[r * vectors : (r + 1) * vectors, :]
        field[outside + r, PAD : PAD + cols, :] = lanes_up(block, jnp.zeros((1, cols), F32))
    terms = (field, odd)
    for k in range(DEGREE):
        tiles = tiles_of(cols, 0)
        bends = advances = tiles
        if k < EARLY:
            bends = [y for y in tiles if y not in tiles_of(cols, 2 * k + 2)]
            advances = [y for y in tiles if y not in tiles_of(cols, 2 * k + 3)]
        operator(k, rows, bends, advances, field, odd, inner, stiff)
        clear_cols(terms[(k + 1) % 2], HALO + 2 + 2 * k, rows - 4 - 4 * k, cols)
    low, high = HALO, rows - HALO
    own = range(PAD, PAD + cols, 8)
    sweep(HALO + low, HALO + high, own, functools.partial(root_bend, terms[DEGREE % 2], stiff, inner))

    first = low + 1
    groups = (high - 1 - first) // GROUP
    sums[...] = jnp.zeros_like(sums)
    final = terms[DEGREE % 2]

    def rows_of(g):
        return [first + g * GROUP + j for j in range(GROUP)]

    def ready(g, slot):
        for j, x in enumerate(rows_of(g)):
            prepare(slot, x, j, vectors, cols, final, inner, turned, lhs)

    ready(0, 0)

    def one(g):
        slot = lax.rem(g, 2)
        multiply(slot, rows_of(g), cols, final, inner, lhs, sums)
        ready(g + 1, 1 - slot)

    loop(groups - 1, one)
    multiply((groups - 1) % 2, rows_of(groups - 1), cols, final, inner, lhs, sums)


def middle(vectors, rows, cols, field, odd, inner, stiff, one):
    big = padded(rows, cols)
    return pl.pallas_call(
        functools.partial(middle_kernel, vectors, rows, cols),
        in_specs=[VMEM] * 5,
        out_specs=[VMEM] * 6,
        out_shape=[
            big,
            big,
            big,
            big,
            jax.ShapeDtypeStruct((rows, vectors, cols), F32),
            jax.ShapeDtypeStruct((2, vectors, 2 * LANES), F32),
        ],
        input_output_aliases={0: 0, 1: 1, 2: 2, 3: 3},
        scratch_shapes=[pltpu.VMEM((2, 2, vectors, GROUP * cols), BF16)],
        compiler_params=params(8),
        cost_estimate=pl.CostEstimate(flops=10**10, bytes_accessed=40 * MIB, transcendentals=0),
    )(field, odd, inner, stiff, one)


def end_kernel(vectors, rows, cols, last, field_in, odd_in, inner_in, stiff_in, turned_in, sums_in,
               *refs):
    if last:
        two, corner, field, odd, inner, stiff, turned, packed, sums, lhs = refs
        corner_at = (HALO - FIRST) * vectors
    else:
        corner, field, odd, inner, stiff, turned, sums, lhs = refs
        corner_at = 0
    row_first = even(lax.axis_index("row"))
    side = jnp.where(row_first, 0 if last else 1, 1 if last else 0)
    base = corner_at + 2 * HALO * MARGIN
    start = side * (HALO + rows)
    for r in range(HALO):
        x = start + r
        weight = corner[base + r : base + r + 1, :]
        if last:
            ref, at = (two, r) if r < FIRST else (corner, r - FIRST)
            block = ref[at * vectors : (at + 1) * vectors, :]
            field[x, PAD : PAD + cols, :] = lanes_up(block, weight)
        stiff[x, PAD : PAD + cols, :] = spread_stiffness(weight)
        for e, y in enumerate((PAD - MARGIN, PAD + cols)):
            at = corner_at + (2 * r + e) * MARGIN
            piece = corner[at : at + MARGIN, :]
            field[x, y : y + MARGIN, :] = piece
            stiff[x, y : y + MARGIN, :] = jnp.broadcast_to(
                piece[:, vectors : vectors + 1] * (2.0 / HALF), (MARGIN, LANES)
            )
    if last:
        clear_rows(field, rows, cols)
        clear_rows(stiff, rows, cols)

    def some_rows(low, ys, work):
        x = low + side * (rows + HALO - 2 * low)
        for y in ys:
            work(x, y, 4)
            work(x + 4, y, HALO - 4)

    terms = (field, odd)
    for k in range(DEGREE):
        current, following = terms[k % 2], terms[(k + 1) % 2]
        low = 1 + 2 * k
        tiles = tiles_of(cols, 0)
        some_rows(low, tiles, functools.partial(bend, current, stiff, inner))
        some_rows(low + 1, tiles, functools.partial(advance, k, current, inner, following))
        clear_cols(following, low + 1 + side * (rows + HALO - 2 * low - 2), HALO, cols)
        if last:
            clear_rows(following, rows, cols)
    final = terms[DEGREE % 2]
    some_rows(HALO, tiles_of(cols, 1), functools.partial(root_bend, final, stiff, inner))

    if last:
        sums[...] = sums_in[...]
    first = side * (rows - HALO - 1)
    for g in range(0, HALO + 1, GROUP):
        xs = [first + x for x in range(g, min(g + GROUP, HALO + 1))]
        for j, x in enumerate(xs):
            prepare(g // GROUP % 2, x, j, vectors, cols, final, inner, turned, lhs)
        multiply(g // GROUP % 2, xs, cols, final, inner, lhs, sums)
    if not last:
        return

    def total(which):
        high, low = sums[which, :, :LANES], sums[which, :, LANES:]
        square = jnp.concatenate([low, jnp.zeros((LANES - vectors, LANES), F32)], axis=0)
        return high + (low + square.T[:vectors])

    gram, image_gram = total(0), total(1)
    i = lax.broadcasted_iota(jnp.int32, (vectors, LANES), 0)
    j = lax.broadcasted_iota(jnp.int32, (vectors, LANES), 1)
    diagonal = jnp.sum(jnp.where(i == j, image_gram, 0.0), axis=1, keepdims=True)
    both_grams = jnp.where(j <= i, gram, image_gram)
    packed[...] = jnp.where(j < vectors, both_grams, jnp.where(j == vectors, diagonal, 0.0))


def end(vectors, rows, cols, state, halo):
    last = len(halo) > 1
    big = padded(rows, cols)
    shapes = [big] * 4 + [jax.ShapeDtypeStruct((rows, vectors, cols), F32)]
    sums = (2, vectors, 2 * LANES)
    shapes.append(jax.ShapeDtypeStruct((vectors, LANES) if last else sums, F32))
    return pl.pallas_call(
        functools.partial(end_kernel, vectors, rows, cols, last),
        in_specs=[VMEM] * (6 + len(halo)),
        out_specs=[VMEM] * 6,
        out_shape=shapes,
        input_output_aliases={i: i for i in range(5 if last else 6)},
        scratch_shapes=([pltpu.VMEM(sums, F32)] if last else [])
        + [pltpu.VMEM((2, 2, vectors, GROUP * cols), BF16)],
        compiler_params=params(8),
    )(*state, *halo)


def inverse_factor(gram, vectors):
    lane = lax.broadcasted_iota(jnp.int32, (8, LANES), 1)
    sub = lax.broadcasted_iota(jnp.int32, (8, LANES), 0)
    count = vectors // 8
    blocks = [gram[8 * b : 8 * b + 8] for b in range(count)]

    def spread(values, j):
        return jnp.broadcast_to(values[:, j : j + 1], (8, LANES))

    done = []
    for b in range(count):
        base = 8 * b
        own = (lane >= base) & (lane < base + 8)
        raw = [jnp.broadcast_to(blocks[b][s : s + 1], (8, LANES)) for s in range(8)]
        pivots = [[spread(raw[s], base + k) if k >= s else None for k in range(8)] for s in range(8)]
        below = {t: [spread(blocks[t], base + k) for k in range(8)] for t in range(b + 1, count)}
        rows = [jnp.where(own, jnp.where(lane == base + s, 1.0, 0.0), raw[s]) for s in range(8)]
        for t in range(b + 1, count):
            blocks[t] = jnp.where(own, 0.0, blocks[t])
        finished = jnp.zeros((8, LANES), F32)
        for s in range(8):
            inverse = 1.0 / pivots[s][s]
            for i in range(s + 1, 8):
                m = pivots[s][i] * inverse
                for k in range(i, 8):
                    pivots[i][k] = pivots[i][k] - m * pivots[s][k]
                rows[i] = rows[i] - m * rows[s]
            finished = jnp.where(sub == s, rows[s] * lax.rsqrt(pivots[s][s]), finished)
            for t in range(b + 1, count):
                q = below[t][s] * inverse
                for k in range(s + 1, 8):
                    below[t][k] = below[t][k] - q * pivots[s][k]
                blocks[t] = blocks[t] - q * rows[s]
        done.append(finished)
    full = jnp.concatenate(done, axis=0)
    i = lax.broadcasted_iota(jnp.int32, (vectors, LANES), 0)
    j = lax.broadcasted_iota(jnp.int32, (vectors, LANES), 1)
    return jnp.where(j <= i, full, 0.0)


def finish_kernel(scale, sums_ref, turned, basis_ref, projected_ref, basis, out_sems):
    rows, vectors, cols = turned.shape
    packed = sums_ref[...]
    i = lax.broadcasted_iota(jnp.int32, (vectors, LANES), 0)
    j = lax.broadcasted_iota(jnp.int32, (vectors, LANES), 1)
    square = jnp.concatenate([packed, jnp.zeros((LANES - vectors, LANES), F32)], axis=0)
    flipped = square.T[:vectors]
    gram = jnp.where(j <= i, packed, flipped)
    inverse = inverse_factor(jnp.where(j < vectors, gram, 0.0), vectors)

    high, low = split(inverse[:, :vectors] * scale)
    group = 8
    copies = []
    for x in range(0, rows, group):
        found = []
        for g in range(0, group, 2):
            pair = jnp.concatenate([turned[x + g], turned[x + g + 1]], axis=1)
            pair_high, pair_low = split(pair)
            result = jnp.dot(high, pair_low, preferred_element_type=F32)
            result += jnp.dot(low, pair_high, preferred_element_type=F32)
            result += jnp.dot(high, pair_high, preferred_element_type=F32)
            found += [result[:, :cols], result[:, cols:]]
        basis[:, x : x + group, :] = jnp.swapaxes(jnp.stack(found), 0, 1)
        copies.append(
            pltpu.make_async_copy(
                basis.at[:, pl.ds(x, group), :], basis_ref.at[:, pl.ds(x, group), :], out_sems.at[x // group]
            )
        )
        copies[-1].start()

    image_gram = jnp.where(j > i, packed, jnp.where(j < i, flipped, packed[:, vectors : vectors + 1]))
    image_gram = jnp.where(j < vectors, image_gram, 0.0)
    half = jnp.dot(
        inverse[:, :vectors], image_gram, preferred_element_type=F32, precision=lax.Precision.HIGHEST
    )
    sandwich = lax.dot_general(
        half, inverse, (((1,), (1,)), ((), ())), preferred_element_type=F32, precision=lax.Precision.HIGHEST
    )
    k = lax.broadcasted_iota(jnp.int32, (vectors, vectors), 0)
    m = lax.broadcasted_iota(jnp.int32, (vectors, vectors), 1)
    projected_ref[...] = sandwich * (HALF / (2.0 * TOP)) + jnp.where(k == m, SHIFT / TOP, 0.0)
    for copy in copies:
        copy.wait()


def finish(sums, turned, scale):
    rows, vectors, cols = turned.shape
    return pl.pallas_call(
        functools.partial(finish_kernel, scale),
        in_specs=[VMEM, VMEM],
        out_specs=[HBM, VMEM],
        out_shape=[
            jax.ShapeDtypeStruct((vectors, rows, cols), F32),
            jax.ShapeDtypeStruct((vectors, vectors), F32),
        ],
        scratch_shapes=[
            pltpu.VMEM((vectors, rows, cols), F32),
            pltpu.SemaphoreType.DMA((rows // 8,)),
        ],
        compiler_params=params(8),
    )(sums, turned)


def pairs(count, start):
    found = []
    for i in range(start, start + count - 1, 2):
        found += [(i % count, (i + 1) % count), ((i + 1) % count, i % count)]
    return found


def inner_pairs(row_count, col_count):
    found = []
    for r in range(row_count):
        for c in range(col_count):
            beside = c + 1 if c % 2 else c - 1
            there = (r, beside) if 0 <= beside < col_count else (r ^ (row_count // 2), c)
            found.append((r * col_count + c, there[0] * col_count + there[1]))
    return found


def all_sum(values, axes):
    count = 1
    for axis in axes:
        count *= lax.axis_size(axis)
    if count & (count - 1):
        return lax.psum(values, axes)
    step = 1
    while step < count:
        values = values + lax.ppermute(values, axes, [(i, i ^ (step | 1)) for i in range(count)])
        step *= 2
    return values


def body(start_block, stiffness):
    vectors, rows, cols = start_block.shape
    row_count, col_count = lax.axis_size("row"), lax.axis_size("col")
    field, near, far, one, two, rest, stiffness = turn(start_block, stiffness)
    near = lax.ppermute(near, "col", pairs(col_count, 0))
    far = lax.ppermute(far, ("row", "col"), inner_pairs(row_count, col_count))
    one = lax.ppermute(one, "row", pairs(row_count, 0))
    two = lax.ppermute(two, "row", pairs(row_count, 1))
    field, stiff, odd, inner = early(field, stiffness)
    field, stiff, corner_one, whole = corners(vectors, field, stiff, stiffness, near, far, rest)
    corner_one = lax.ppermute(corner_one, "row", pairs(row_count, 0))
    whole = lax.ppermute(whole, "row", pairs(row_count, 1))
    state = middle(vectors, rows, cols, field, odd, inner, stiff, one)
    state = end(vectors, rows, cols, state, (corner_one,))
    *_, turned, sums = end(vectors, rows, cols, state, (two, whole))
    sums = all_sum(sums, ("row", "col"))
    scale = float(rows * row_count * cols * col_count) ** 0.5
    return tuple(finish(sums, turned, scale))


def solution(mesh):
    in_specs = (P(None, "row", "col"), P("row", "col"))
    out_specs = (P(None, "row", "col"), P())
    return jax.shard_map(body, mesh=mesh, in_specs=in_specs, out_specs=out_specs, check_vma=False)
```

```python
import functools
import jax
import jax.numpy as jnp
from jax import lax
from jax.experimental import pallas as pl
from jax.experimental.pallas import tpu as pltpu
from jax.sharding import PartitionSpec as P

DEGREE = 4
TOP = 129.0
CUT = 16.0
SHIFT = 1.0
CENTER = (TOP + CUT) / 2.0
HALF = (TOP - CUT) / 2.0
LEAD = (CENTER - SHIFT) / HALF
HALO = 2 * DEGREE + 1
MARGIN = HALO - 1
FIRST = 5
EARLY = 3
LANES = 128
PAD = 16
GROUP = 4
F32 = jnp.float32
BF16 = jnp.bfloat16
MIB = 2**20
VMEM = pl.BlockSpec(memory_space=pltpu.VMEM)
HBM = pl.BlockSpec(memory_space=pltpu.HBM)


def split(values):
    high = values.astype(BF16)
    low = (values - high.astype(F32)).astype(BF16)
    return high, low


def even(index):
    return lax.rem(index, 2) == 0


def loop(count, work):
    def one(i, carry):
        work(i)
        return carry

    lax.fori_loop(0, count, one, 0)


def params(limit):
    return pltpu.CompilerParams(vmem_limit_bytes=limit * MIB)


def padded(rows, cols):
    return jax.ShapeDtypeStruct((rows + 2 * HALO, cols + 2 * PAD, LANES), F32)


def lanes_up(block, stiff):
    vectors, cols = block.shape
    fill = jnp.zeros((LANES - vectors - 8, cols), F32)
    return jnp.concatenate([block, jnp.broadcast_to(stiff, (8, cols)), fill], axis=0).T


def spread_stiffness(row):
    return jnp.broadcast_to(row * (2.0 / HALF), (LANES, row.shape[1])).T


def turn_kernel(block_ref, stiff_ref, field, near, far, one, two, rest, stiff, held, sems, slab_sems):
    chunks, vectors, step, cols = held.shape
    rows = chunks * step
    col_first, row_first = even(lax.axis_index("col")), even(lax.axis_index("row"))
    stiff_copy = pltpu.make_async_copy(stiff_ref, stiff, sems.at[chunks])
    copies = [
        pltpu.make_async_copy(block_ref.at[:, pl.ds(i * step, step), :], held.at[i], sems.at[i])
        for i in range(chunks)
    ]
    slab_copies = []
    for which, start in enumerate(
        (jnp.where(row_first, rows - HALO, 0), jnp.where(row_first, 0, rows - HALO))
    ):
        for r in range(HALO):
            out, at = (one, r) if which == 0 else (two, r) if r < FIRST else (rest, r - FIRST)
            slab_copies.append(
                pltpu.make_async_copy(
                    block_ref.at[:, start + r, :], out.at[pl.ds(at * vectors, vectors), :], slab_sems.at[which, r]
                )
            )
    for copy in [stiff_copy] + copies + slab_copies:
        copy.start()
    stiff_copy.wait()
    for i in range(chunks):
        copies[i].wait()
        for r in range(step):
            x = i * step + r
            if r % 8 == 0:
                eight = jnp.swapaxes(held[i, :, r : r + 8, :], 0, 1)
            turned = lanes_up(eight[r % 8], stiff[x : x + 1, :])
            field[HALO + x, PAD : PAD + cols, :] = turned
            head, tail = turned[:HALO], turned[cols - HALO :]
            near[x * HALO : (x + 1) * HALO, :] = jnp.where(col_first, tail, head)
            far[x * HALO : (x + 1) * HALO, :] = jnp.where(col_first, head, tail)
    for copy in slab_copies:
        copy.wait()


def turn(block, stiffness):
    vectors, rows, cols = block.shape
    side = jax.ShapeDtypeStruct((rows * HALO, LANES), F32)

    def slab(count):
        return jax.ShapeDtypeStruct((count * vectors, cols), F32)

    step = 16
    return pl.pallas_call(
        turn_kernel,
        in_specs=[HBM] * 2,
        out_specs=[VMEM] * 7,
        out_shape=[
            padded(rows, cols),
            side,
            side,
            slab(HALO),
            slab(FIRST),
            slab(HALO - FIRST),
            jax.ShapeDtypeStruct(stiffness.shape, F32),
        ],
        scratch_shapes=[
            pltpu.VMEM((rows // step, vectors, step, cols), F32),
            pltpu.SemaphoreType.DMA((rows // step + 1,)),
            pltpu.SemaphoreType.DMA((2, HALO)),
        ],
        compiler_params=params(8),
        cost_estimate=pl.CostEstimate(flops=0, bytes_accessed=4 * vectors * rows * cols * 2, transcendentals=0),
    )(
        pltpu.with_memory_space_constraint(block, pltpu.HBM),
        pltpu.with_memory_space_constraint(stiffness, pltpu.HBM),
    )


def corner_kernel(vectors, field_in, stiff_in, stiff_ref, near, far, rest, field, stiff, one, whole):
    rows, cols = stiff_ref.shape
    col_first, row_first = even(lax.axis_index("col")), even(lax.axis_index("row"))
    left = jnp.where(lax.axis_index("col") == 0, 0.0, 1.0)
    right = jnp.where(lax.axis_index("col") == lax.axis_size("col") - 1, 0.0, 1.0)
    step = 8
    ends = (PAD - MARGIN, PAD + cols)

    def some(i):
        for r in range(step):
            x = i * step + r
            a, b = near[pl.ds(x * HALO, HALO), :], far[pl.ds(x * HALO, HALO), :]
            field[HALO + x, PAD - HALO : PAD, :] = jnp.where(col_first, b, a) * left
            field[HALO + x, PAD + cols : PAD + cols + HALO, :] = jnp.where(col_first, a, b) * right
        for r in range(step):
            x = HALO + i * step + r
            for y in ends:
                lane = field[x, y : y + MARGIN, vectors : vectors + 1] * (2.0 / HALF)
                stiff[x, y : y + MARGIN, :] = jnp.broadcast_to(lane, (MARGIN, LANES))

    loop(rows // step, some)
    last = rows - HALO
    size = rest.shape[0]
    whole[:size, :] = rest[...]
    two = whole.at[size:, :]
    for out, start in ((one, jnp.where(row_first, last, 0)), (two, jnp.where(row_first, 0, last))):
        for r in range(HALO):
            for e, y in enumerate(ends):
                out[(2 * r + e) * MARGIN : (2 * r + e + 1) * MARGIN, :] = field[HALO + start + r, y : y + MARGIN, :]
        base = 2 * HALO * MARGIN
        out[base:, :] = jnp.zeros((out.shape[0] - base, LANES), F32)
    base = 2 * HALO * MARGIN
    head, tail = stiff_ref[:HALO, :], stiff_ref[last:, :]
    one[base : base + HALO, :] = jnp.where(row_first, tail, head)
    two[base : base + HALO, :] = jnp.where(row_first, head, tail)


def corners(vectors, field, stiff, stiffness, near, far, rest):
    rows, cols = stiffness.shape
    corner = jax.ShapeDtypeStruct((2 * HALO * MARGIN + 16, LANES), F32)
    whole = jax.ShapeDtypeStruct((rest.shape[0] + corner.shape[0], LANES), F32)
    return pl.pallas_call(
        functools.partial(corner_kernel, vectors),
        in_specs=[VMEM] * 6,
        out_specs=[VMEM] * 4,
        out_shape=[padded(rows, cols), padded(rows, cols), corner, whole],
        input_output_aliases={0: 0, 1: 1},
        compiler_params=params(4),
        cost_estimate=pl.CostEstimate(flops=0, bytes_accessed=0, transcendentals=0),
    )(field, stiff, stiffness, near, far, rest)


def around(ref, x, y, step):
    mid = ref[pl.ds(x - 1, step + 2), pl.ds(y, 8), :]
    left = ref[pl.ds(x, step), pl.ds(y - 1, 8), :]
    right = ref[pl.ds(x, step), pl.ds(y + 1, 8), :]
    return ((mid[:-2] + mid[2:]) + (left + right)) - 4.0 * mid[1:-1]


def bend(field, stiff, inner, x, y, step):
    at = (pl.ds(x, step), pl.ds(y, 8))
    inner[*at, :] = stiff[*at, :] * around(field, x, y, step)


def advance(k, current, inner, following, x, y, step):
    at = (pl.ds(x, step), pl.ds(y, 8))
    image = around(inner, x, y, step)
    here = current[*at, :]
    if k == 0:
        following[*at, :] = LEAD * here - 0.5 * image
    else:
        following[*at, :] = (2.0 * LEAD * here - following[*at, :]) - image


def root_bend(field, stiff, inner, x, y, step):
    at = (pl.ds(x, step), pl.ds(y, 8))
    weight = stiff[*at, :]
    inner[*at, :] = weight * lax.rsqrt(weight) * around(field, x, y, step)


def sweep(low, high, ys, work):
    step, unroll = 4, 4

    def trip(i):
        for u in range(unroll):
            for y in ys:
                work(low + (i * unroll + u) * step, y, step)

    trips = (high - low) // (step * unroll)
    loop(trips, trip)
    for x in range(low + trips * unroll * step, high, step):
        for y in ys:
            work(x, y, min(step, high - x))


def clear_cols(field, low, height, cols):
    col, count = lax.axis_index("col"), lax.axis_size("col")

    def at(start):
        field[pl.ds(low, height), start : start + MARGIN, :] = jnp.zeros((height, MARGIN, LANES), F32)

    pl.when(col == 0)(lambda: at(PAD - MARGIN))
    pl.when(col == count - 1)(lambda: at(PAD + cols))


def clear_rows(field, rows, cols):
    row, count = lax.axis_index("row"), lax.axis_size("row")

    def at(start):
        wide = cols + 2 * MARGIN
        for x in range(start, start + HALO):
            field[x, PAD - MARGIN : PAD + cols + MARGIN, :] = jnp.zeros((wide, LANES), F32)

    pl.when(row == 0)(lambda: at(0))
    pl.when(row == count - 1)(lambda: at(HALO + rows))


def tiles_of(cols, inset):
    return range(PAD - MARGIN + 8 * inset, PAD + cols + MARGIN - 8 * inset, 8)


def operator(k, rows, bends, advances, field, odd, inner, stiff):
    current, following = ((field, odd), (odd, field))[k % 2]
    low, high = HALO + 1 + 2 * k, HALO + rows - 1 - 2 * k
    sweep(low, high, bends, functools.partial(bend, current, stiff, inner))
    sweep(low + 1, high - 1, advances, functools.partial(advance, k, current, inner, following))


def early_kernel(field_in, stiff_ref, field, stiff, odd, inner):
    rows, cols = stiff_ref.shape
    step = 32

    def some(i):
        for r in range(step):
            x = i * step + r
            stiff[HALO + x, PAD : PAD + cols, :] = spread_stiffness(stiff_ref[pl.ds(x, 1), :])

    loop(rows // step, some)
    for k in range(EARLY):
        operator(k, rows, tiles_of(cols, 2 * k + 2), tiles_of(cols, 2 * k + 3), field, odd, inner, stiff)


def early(field, stiffness):
    rows, cols = stiffness.shape
    big = padded(rows, cols)
    return pl.pallas_call(
        early_kernel,
        in_specs=[VMEM] * 2,
        out_specs=[VMEM] * 4,
        out_shape=[big] * 4,
        input_output_aliases={0: 0},
        compiler_params=params(4),
        cost_estimate=pl.CostEstimate(flops=0, bytes_accessed=0, transcendentals=0),
    )(field, stiffness)


def prepare(slot, x, j, vectors, cols, field, inner, turned, lhs):
    cells = field[HALO + x, PAD : PAD + cols, :].T[:vectors]
    turned[x] = cells
    lhs[slot, 0, :, j * cols : (j + 1) * cols] = cells.astype(BF16)
    lhs[slot, 1, :, j * cols : (j + 1) * cols] = inner[HALO + x, PAD : PAD + cols, :].astype(BF16).T[:vectors]


def multiply(slot, xs, cols, field, inner, lhs, sums):
    width = len(xs) * cols
    for which, ref in enumerate((field, inner)):
        cells = jnp.concatenate([ref[HALO + x, PAD : PAD + cols, :] for x in xs], axis=0)
        high, low = split(cells)
        sums[which] += jnp.dot(
            lhs[slot, which, :, :width], jnp.concatenate([high, low], axis=1), preferred_element_type=F32
        )


def middle_kernel(vectors, rows, cols, field_in, odd_in, inner_in, stiff_in, one, field, odd, inner, stiff, turned, sums, lhs):
    outside = jnp.where(even(lax.axis_index("row")), HALO + rows, 0)
    for r in range(HALO):
        block = one[r * vectors : (r + 1) * vectors, :]
        field[outside + r, PAD : PAD + cols, :] = lanes_up(block, jnp.zeros((1, cols), F32))
    terms = (field, odd)
    for k in range(DEGREE):
        tiles = tiles_of(cols, 0)
        bends = advances = tiles
        if k < EARLY:
            bends = [y for y in tiles if y not in tiles_of(cols, 2 * k + 2)]
            advances = [y for y in tiles if y not in tiles_of(cols, 2 * k + 3)]
        operator(k, rows, bends, advances, field, odd, inner, stiff)
        clear_cols(terms[(k + 1) % 2], HALO + 2 + 2 * k, rows - 4 - 4 * k, cols)
    low, high = HALO, rows - HALO
    own = range(PAD, PAD + cols, 8)
    sweep(HALO + low, HALO + high, own, functools.partial(root_bend, terms[DEGREE % 2], stiff, inner))

    first = low + 1
    groups = (high - 1 - first) // GROUP
    sums[...] = jnp.zeros_like(sums)
    final = terms[DEGREE % 2]

    def rows_of(g):
        return [first + g * GROUP + j for j in range(GROUP)]

    def ready(g, slot):
        for j, x in enumerate(rows_of(g)):
            prepare(slot, x, j, vectors, cols, final, inner, turned, lhs)

    ready(0, 0)

    def one(g):
        slot = lax.rem(g, 2)
        multiply(slot, rows_of(g), cols, final, inner, lhs, sums)
        ready(g + 1, 1 - slot)

    loop(groups - 1, one)
    multiply((groups - 1) % 2, rows_of(groups - 1), cols, final, inner, lhs, sums)


def middle(vectors, rows, cols, field, odd, inner, stiff, one):
    big = padded(rows, cols)
    return pl.pallas_call(
        functools.partial(middle_kernel, vectors, rows, cols),
        in_specs=[VMEM] * 5,
        out_specs=[VMEM] * 6,
        out_shape=[
            big,
            big,
            big,
            big,
            jax.ShapeDtypeStruct((rows, vectors, cols), F32),
            jax.ShapeDtypeStruct((2, vectors, 2 * LANES), F32),
        ],
        input_output_aliases={0: 0, 1: 1, 2: 2, 3: 3},
        scratch_shapes=[pltpu.VMEM((2, 2, vectors, GROUP * cols), BF16)],
        compiler_params=params(8),
        cost_estimate=pl.CostEstimate(flops=10**10, bytes_accessed=40 * MIB, transcendentals=0),
    )(field, odd, inner, stiff, one)


def end_kernel(vectors, rows, cols, last, field_in, odd_in, inner_in, stiff_in, turned_in, sums_in,
               *refs):
    if last:
        two, corner, field, odd, inner, stiff, turned, packed, sums, lhs = refs
        corner_at = (HALO - FIRST) * vectors
    else:
        corner, field, odd, inner, stiff, turned, sums, lhs = refs
        corner_at = 0
    row_first = even(lax.axis_index("row"))
    side = jnp.where(row_first, 0 if last else 1, 1 if last else 0)
    base = corner_at + 2 * HALO * MARGIN
    start = side * (HALO + rows)
    for r in range(HALO):
        x = start + r
        weight = corner[base + r : base + r + 1, :]
        if last:
            ref, at = (two, r) if r < FIRST else (corner, r - FIRST)
            block = ref[at * vectors : (at + 1) * vectors, :]
            field[x, PAD : PAD + cols, :] = lanes_up(block, weight)
        stiff[x, PAD : PAD + cols, :] = spread_stiffness(weight)
        for e, y in enumerate((PAD - MARGIN, PAD + cols)):
            at = corner_at + (2 * r + e) * MARGIN
            piece = corner[at : at + MARGIN, :]
            field[x, y : y + MARGIN, :] = piece
            stiff[x, y : y + MARGIN, :] = jnp.broadcast_to(
                piece[:, vectors : vectors + 1] * (2.0 / HALF), (MARGIN, LANES)
            )
    if last:
        clear_rows(field, rows, cols)
        clear_rows(stiff, rows, cols)

    def some_rows(low, ys, work):
        x = low + side * (rows + HALO - 2 * low)
        for y in ys:
            work(x, y, 4)
            work(x + 4, y, HALO - 4)

    terms = (field, odd)
    for k in range(DEGREE):
        current, following = terms[k % 2], terms[(k + 1) % 2]
        low = 1 + 2 * k
        tiles = tiles_of(cols, 0)
        some_rows(low, tiles, functools.partial(bend, current, stiff, inner))
        some_rows(low + 1, tiles, functools.partial(advance, k, current, inner, following))
        clear_cols(following, low + 1 + side * (rows + HALO - 2 * low - 2), HALO, cols)
        if last:
            clear_rows(following, rows, cols)
    final = terms[DEGREE % 2]
    some_rows(HALO, tiles_of(cols, 1), functools.partial(root_bend, final, stiff, inner))

    if last:
        sums[...] = sums_in[...]
    first = side * (rows - HALO - 1)
    for g in range(0, HALO + 1, GROUP):
        xs = [first + x for x in range(g, min(g + GROUP, HALO + 1))]
        for j, x in enumerate(xs):
            prepare(g // GROUP % 2, x, j, vectors, cols, final, inner, turned, lhs)
        multiply(g // GROUP % 2, xs, cols, final, inner, lhs, sums)
    if not last:
        return

    def total(which):
        high, low = sums[which, :, :LANES], sums[which, :, LANES:]
        square = jnp.concatenate([low, jnp.zeros((LANES - vectors, LANES), F32)], axis=0)
        return high + (low + square.T[:vectors])

    gram, image_gram = total(0), total(1)
    i = lax.broadcasted_iota(jnp.int32, (vectors, LANES), 0)
    j = lax.broadcasted_iota(jnp.int32, (vectors, LANES), 1)
    diagonal = jnp.sum(jnp.where(i == j, image_gram, 0.0), axis=1, keepdims=True)
    both_grams = jnp.where(j <= i, gram, image_gram)
    packed[...] = jnp.where(j < vectors, both_grams, jnp.where(j == vectors, diagonal, 0.0))


def end(vectors, rows, cols, state, halo):
    last = len(halo) > 1
    big = padded(rows, cols)
    shapes = [big] * 4 + [jax.ShapeDtypeStruct((rows, vectors, cols), F32)]
    sums = (2, vectors, 2 * LANES)
    shapes.append(jax.ShapeDtypeStruct((vectors, LANES) if last else sums, F32))
    return pl.pallas_call(
        functools.partial(end_kernel, vectors, rows, cols, last),
        in_specs=[VMEM] * (6 + len(halo)),
        out_specs=[VMEM] * 6,
        out_shape=shapes,
        input_output_aliases={i: i for i in range(5 if last else 6)},
        scratch_shapes=([pltpu.VMEM(sums, F32)] if last else [])
        + [pltpu.VMEM((2, 2, vectors, GROUP * cols), BF16)],
        compiler_params=params(8),
    )(*state, *halo)


def inverse_factor(gram, vectors):
    lane = lax.broadcasted_iota(jnp.int32, (8, LANES), 1)
    sub = lax.broadcasted_iota(jnp.int32, (8, LANES), 0)
    count = vectors // 8
    blocks = [gram[8 * b : 8 * b + 8] for b in range(count)]

    def spread(values, j):
        return jnp.broadcast_to(values[:, j : j + 1], (8, LANES))

    done = []
    for b in range(count):
        base = 8 * b
        own = (lane >= base) & (lane < base + 8)
        raw = [jnp.broadcast_to(blocks[b][s : s + 1], (8, LANES)) for s in range(8)]
        pivots = [[spread(raw[s], base + k) if k >= s else None for k in range(8)] for s in range(8)]
        below = {t: [spread(blocks[t], base + k) for k in range(8)] for t in range(b + 1, count)}
        rows = [jnp.where(own, jnp.where(lane == base + s, 1.0, 0.0), raw[s]) for s in range(8)]
        for t in range(b + 1, count):
            blocks[t] = jnp.where(own, 0.0, blocks[t])
        finished = jnp.zeros((8, LANES), F32)
        for s in range(8):
            inverse = 1.0 / pivots[s][s]
            for i in range(s + 1, 8):
                m = pivots[s][i] * inverse
                for k in range(i, 8):
                    pivots[i][k] = pivots[i][k] - m * pivots[s][k]
                rows[i] = rows[i] - m * rows[s]
            finished = jnp.where(sub == s, rows[s] * lax.rsqrt(pivots[s][s]), finished)
            for t in range(b + 1, count):
                q = below[t][s] * inverse
                for k in range(s + 1, 8):
                    below[t][k] = below[t][k] - q * pivots[s][k]
                blocks[t] = blocks[t] - q * rows[s]
        done.append(finished)
    full = jnp.concatenate(done, axis=0)
    i = lax.broadcasted_iota(jnp.int32, (vectors, LANES), 0)
    j = lax.broadcasted_iota(jnp.int32, (vectors, LANES), 1)
    return jnp.where(j <= i, full, 0.0)


def finish_kernel(scale, sums_ref, turned, basis_ref, projected_ref, basis, out_sems):
    rows, vectors, cols = turned.shape
    packed = sums_ref[...]
    i = lax.broadcasted_iota(jnp.int32, (vectors, LANES), 0)
    j = lax.broadcasted_iota(jnp.int32, (vectors, LANES), 1)
    square = jnp.concatenate([packed, jnp.zeros((LANES - vectors, LANES), F32)], axis=0)
    flipped = square.T[:vectors]
    gram = jnp.where(j <= i, packed, flipped)
    inverse = inverse_factor(jnp.where(j < vectors, gram, 0.0), vectors)

    high, low = split(inverse[:, :vectors] * scale)
    group = 8
    copies = []
    for x in range(0, rows, group):
        found = []
        for g in range(0, group, 2):
            pair = jnp.concatenate([turned[x + g], turned[x + g + 1]], axis=1)
            pair_high, pair_low = split(pair)
            result = jnp.dot(high, pair_low, preferred_element_type=F32)
            result += jnp.dot(low, pair_high, preferred_element_type=F32)
            result += jnp.dot(high, pair_high, preferred_element_type=F32)
            found += [result[:, :cols], result[:, cols:]]
        basis[:, x : x + group, :] = jnp.swapaxes(jnp.stack(found), 0, 1)
        copies.append(
            pltpu.make_async_copy(
                basis.at[:, pl.ds(x, group), :], basis_ref.at[:, pl.ds(x, group), :], out_sems.at[x // group]
            )
        )
        copies[-1].start()

    image_gram = jnp.where(j > i, packed, jnp.where(j < i, flipped, packed[:, vectors : vectors + 1]))
    image_gram = jnp.where(j < vectors, image_gram, 0.0)
    half = jnp.dot(
        inverse[:, :vectors], image_gram, preferred_element_type=F32, precision=lax.Precision.HIGHEST
    )
    sandwich = lax.dot_general(
        half, inverse, (((1,), (1,)), ((), ())), preferred_element_type=F32, precision=lax.Precision.HIGHEST
    )
    k = lax.broadcasted_iota(jnp.int32, (vectors, vectors), 0)
    m = lax.broadcasted_iota(jnp.int32, (vectors, vectors), 1)
    projected_ref[...] = sandwich * (HALF / (2.0 * TOP)) + jnp.where(k == m, SHIFT / TOP, 0.0)
    for copy in copies:
        copy.wait()


def finish(sums, turned, scale):
    rows, vectors, cols = turned.shape
    return pl.pallas_call(
        functools.partial(finish_kernel, scale),
        in_specs=[VMEM, VMEM],
        out_specs=[HBM, VMEM],
        out_shape=[
            jax.ShapeDtypeStruct((vectors, rows, cols), F32),
            jax.ShapeDtypeStruct((vectors, vectors), F32),
        ],
        scratch_shapes=[
            pltpu.VMEM((vectors, rows, cols), F32),
            pltpu.SemaphoreType.DMA((rows // 8,)),
        ],
        compiler_params=params(8),
    )(sums, turned)


def pairs(count, start):
    found = []
    for i in range(start, start + count - 1, 2):
        found += [(i % count, (i + 1) % count), ((i + 1) % count, i % count)]
    return found


def inner_pairs(row_count, col_count):
    found = []
    for r in range(row_count):
        for c in range(col_count):
            beside = c + 1 if c % 2 else c - 1
            there = (r, beside) if 0 <= beside < col_count else (r ^ (row_count // 2), c)
            found.append((r * col_count + c, there[0] * col_count + there[1]))
    return found


def all_sum(values, axes):
    count = 1
    for axis in axes:
        count *= lax.axis_size(axis)
    if count & (count - 1):
        return lax.psum(values, axes)
    step = 1
    while step < count:
        values = values + lax.ppermute(values, axes, [(i, i ^ (step | 1)) for i in range(count)])
        step *= 2
    return values


def body(start_block, stiffness):
    vectors, rows, cols = start_block.shape
    row_count, col_count = lax.axis_size("row"), lax.axis_size("col")
    field, near, far, one, two, rest, stiffness = turn(start_block, stiffness)
    near = lax.ppermute(near, "col", pairs(col_count, 0))
    far = lax.ppermute(far, ("row", "col"), inner_pairs(row_count, col_count))
    one = lax.ppermute(one, "row", pairs(row_count, 0))
    two = lax.ppermute(two, "row", pairs(row_count, 1))
    field, stiff, odd, inner = early(field, stiffness)
    field, stiff, corner_one, whole = corners(vectors, field, stiff, stiffness, near, far, rest)
    corner_one = lax.ppermute(corner_one, "row", pairs(row_count, 0))
    whole = lax.ppermute(whole, "row", pairs(row_count, 1))
    state = middle(vectors, rows, cols, field, odd, inner, stiff, one)
    state = end(vectors, rows, cols, state, (corner_one,))
    *_, turned, sums = end(vectors, rows, cols, state, (two, whole))
    sums = all_sum(sums, ("row", "col"))
    scale = float(rows * row_count * cols * col_count) ** 0.5
    return tuple(finish(sums, turned, scale))


def solution(mesh):
    in_specs = (P(None, "row", "col"), P("row", "col"))
    out_specs = (P(None, "row", "col"), P())
    return jax.shard_map(body, mesh=mesh, in_specs=in_specs, out_specs=out_specs, check_vma=False)
```
